128 devices in a mesh: tm: 32 (over x, z, core), band: 4 (over y).
Axes of the slice: x: 4, y: 4, z: 4, core: 2. Of those that a mesh axis runs over, the one named last changes fastest.
Arguments:
- frames_in: bfloat16 [64, 32, 256, 128], P('tm', 'band'), may hold values from -6 to 6
- clip_id: int32 [64], replicated, may hold values from 0 to 15, never falling along the last dimension, each value on 1 to 16 neighbouring positions
- conv_weight: bfloat16 [3, 3, 3, 128, 128], replicated, may hold values from -0.109375 to 0.109375
- conv_bias: float32 [128], replicated, may hold values from -3 to 3
- norm_gain: float32 [128], replicated, may hold values from 0.1 to 1.9
- norm_shift: float32 [128], replicated, may hold values from -3 to 3
- down_weight: bfloat16 [3, 3, 3, 128, 256], replicated, may hold values from -0.109375 to 0.109375
- out_gain: float32 [256], replicated, may hold values from 0.1 to 1.9
- out_shift: float32 [256], replicated, may hold values from -3 to 3
Outputs:
- encoded: bfloat16 [64, 16, 128, 256], P('tm', 'band')
The draws below stay inside these ranges and needn't reach their ends.
Inputs may be any that keep to these rules, and one draw needn't show every extreme that they name: `clip_id`: clip numbers never fall along the frames; every clip covers 1 to 16 consecutive frames and one covers exactly 16.
All inputs are finite; a program needn't handle non-finite values.
Results may differ from the reference program's by a relative error of at most 0.011.
Values may be sent and summed in bfloat16 or wider, within the bound.
No kernel may reach another device: no remote copies, remote signals or barrier semaphores. Data moves between devices by JAX's collectives and lax.ppermute only.
A program may use at most 64 MiB of HBM per device.

```python
import math
import jax
import jax.numpy as jnp
import numpy as np
from jax import lax

CH = 128
CH2 = 256
GROUPS = 32
COLS = 256
FRAMES = 64
HEIGHT = 32
CLIPS = 16
MOST_LEN = 16


def block_levels(stream_key, extent, split, least, high):
    def one(dim, blocks):
        draws = jax.random.uniform(jax.random.fold_in(jax.random.fold_in(stream_key, 6), dim), (blocks,), jnp.float32, least / len(split), high / len(split))
        return jnp.repeat(jnp.exp(draws), extent[dim] // blocks).reshape((-1,) + (1,) * (len(extent) - dim - 1))

    factor_of = one(*split[0])
    for cut in split[1:]:
        factor_of = factor_of * one(*cut)
    return factor_of


def profile(count, total, bound, slope):
    weights = [(1 << 20) // math.isqrt(rank ** slope) + 1 for rank in range(2, count + 1)]
    spare, given = total - bound - (count - 1), [1] * (count - 1)
    while spare > 0:
        candidates = [i for i in range(count - 1) if given[i] < bound]
        whole, remaining = sum([weights[i] for i in candidates]), spare
        for i in candidates:
            more = min(bound - given[i], max(1, remaining * weights[i] // whole), spare)
            given[i] = given[i] + more
            spare = spare - more
    return np.array([bound] + given)


def uneven(stream_key, amount, total, bound, slope):
    if amount == 2:
        one = jax.random.randint(stream_key, (), max(1, total - bound), min(bound, total - 1) + 1)
        return jnp.stack([one, total - one])
    tallies = jnp.asarray(profile(amount, total, bound, slope), jnp.int32)
    twos = (amount - 1) // 2
    donor, receiver = tallies[1:1 + 2 * twos:2], tallies[2:2 + 2 * twos:2]
    room = jnp.minimum(donor - 1, bound - receiver)
    passed = jax.random.randint(jax.random.fold_in(stream_key, 1), (twos,), 0, 1 << 20) % (room + 1)
    tallies = tallies.at[1:1 + 2 * twos:2].set(donor - passed).at[2:2 + 2 * twos:2].set(receiver + passed)
    return tallies[jax.random.permutation(jax.random.fold_in(stream_key, 2), amount)]


def gaussian(key, shape, spread, limit, pieces=(), held_as=jnp.bfloat16):
    drawn = spread * jax.random.normal(key, shape, jnp.float32)
    if pieces:
        drawn = drawn * block_levels(key, shape, pieces, -0.22, 0.18)
    return jnp.clip(drawn, -limit, limit).astype(held_as)


def setup_inputs(seed: int = 0) -> dict:
    key_of = jax.random.split(jax.random.key(seed), 10)
    return {
        "frames_in": gaussian(key_of[0], (FRAMES, HEIGHT, COLS, CH), 1.0, 6.0, ((0, 32), (1, 4))),
        "clip_id": jnp.searchsorted(jnp.cumsum(uneven(key_of[1], CLIPS, FRAMES, MOST_LEN, 2)), jnp.arange(FRAMES), side="right").astype(jnp.int32),
        "conv_weight": gaussian(key_of[2], (3, 3, 3, CH, CH), (27 * CH) ** -0.5, 0.109375),
        "conv_bias": gaussian(key_of[3], (CH,), 0.5, 3.0, (), jnp.float32),
        "norm_gain": jnp.clip(1.0 + 0.18 * jax.random.normal(key_of[4], (CH,), jnp.float32), 0.1, 1.9),
        "norm_shift": gaussian(key_of[5], (CH,), 0.5, 3.0, (), jnp.float32),
        "down_weight": gaussian(key_of[6], (3, 3, 3, CH, CH2), (27 * CH) ** -0.5, 0.109375),
        "out_gain": jnp.clip(1.0 + 0.18 * jax.random.normal(key_of[7], (CH2,), jnp.float32), 0.1, 1.9),
        "out_shift": gaussian(key_of[8], (CH2,), 0.5, 3.0, (), jnp.float32),
    }


EPS = 1e-06
TAP_PAIRS = ((0, 0), (0, 1), (1, 0))

def frame_sums(frames, groups):
    values = frames.astype(jnp.float32).reshape(-1, groups, frames.shape[-1] // groups)
    return (lax.optimization_barrier(jnp.sum(values, axis=(0, 2))), lax.optimization_barrier(jnp.sum(values * values, axis=(0, 2))))

def clip_moments(stacked, clip_id, groups):
    sums_one, sums_two = lax.map(lambda frames: frame_sums(frames, groups), stacked)
    same_clip = (clip_id[:, None] == clip_id[None, :]).astype(jnp.float32)
    total_one = jnp.dot(same_clip, sums_one, precision=lax.Precision.HIGHEST)
    total_two = jnp.dot(same_clip, sums_two, precision=lax.Precision.HIGHEST)
    cells = float(stacked.shape[1] * stacked.shape[2] * (stacked.shape[3] // groups))
    cell_count = lax.optimization_barrier(jnp.sum(same_clip, axis=1)) * cells
    average = total_one / cell_count[:, None]
    inv_std = lax.rsqrt(total_two / cell_count[:, None] - average * average + EPS)
    return (average, inv_std)

def normalize(frames, average, inv_std, gain, offset):
    repeat = frames.shape[-1] // average.shape[-1]
    centred = frames.astype(jnp.float32) - jnp.repeat(average, repeat)
    return centred * jnp.repeat(inv_std, repeat) * gain + offset

def conv_same(stacked, weight):
    row_count, col_count, channels = (stacked.shape[1], stacked.shape[2], stacked.shape[3])
    padded = jnp.pad(stacked, ((0, 0), (1, 1), (1, 1), (0, 0)))
    summed = jnp.zeros((row_count * col_count, weight.shape[-1]), jnp.float32)
    for tap_t in range(3):
        for tap_y in range(3):
            for tap_x in range(3):
                window = padded[tap_t, tap_y:tap_y + row_count, tap_x:tap_x + col_count].reshape(-1, channels)
                summed = summed + jnp.dot(window, weight[tap_t, tap_y, tap_x], preferred_element_type=jnp.float32)
    return summed.reshape(row_count, col_count, -1)

def conv_down(stacked, weight):
    row_count, col_count, channels = (stacked.shape[1], stacked.shape[2], stacked.shape[3])
    half_rows, half_cols = (row_count // 2, col_count // 2)
    padded = jnp.pad(stacked, ((0, 0), (0, 2), (0, 2), (0, 0)))
    strided = padded.reshape(3, half_rows + 1, 2, half_cols + 1, 2, channels)
    summed = jnp.zeros((half_rows * half_cols, weight.shape[-1]), jnp.float32)
    for tap_t in range(3):
        for tap_y, (row_block, row_phase) in enumerate(TAP_PAIRS):
            for tap_x, (col_block, col_phase) in enumerate(TAP_PAIRS):
                window = strided[tap_t, row_block:row_block + half_rows, row_phase, col_block:col_block + half_cols, col_phase]
                summed = summed + jnp.dot(window.reshape(-1, channels), weight[tap_t, tap_y, tap_x], preferred_element_type=jnp.float32)
    return summed.reshape(half_rows, half_cols, -1)

def reference(frames_in, clip_id, conv_weight, conv_bias, norm_gain, norm_shift, down_weight, out_gain, out_shift):
    frame_count = frames_in.shape[0]
    average, inv_std = clip_moments(frames_in, clip_id, GROUPS)
    hidden = lax.map(lambda item: jax.nn.silu(normalize(item[0], item[1], item[2], norm_gain, norm_shift)).astype(jnp.bfloat16), (frames_in, average, inv_std))
    clip_start = lax.optimization_barrier(jnp.sum((clip_id[None, :] < clip_id[:, None]).astype(jnp.int32), axis=1))

    def sources(index):
        return jnp.maximum(jnp.arange(3, dtype=jnp.int32) + index - 2, clip_start[index]).astype(jnp.int32)

    def first_section(index):
        stacked = jnp.take(hidden, sources(index), axis=0)
        return (frames_in[index].astype(jnp.float32) + conv_same(stacked, conv_weight) + conv_bias).astype(jnp.bfloat16)
    frame_index = jnp.arange(frame_count, dtype=jnp.int32)
    residual = lax.map(first_section, frame_index)

    def second_section(index):
        return conv_down(jnp.take(residual, sources(index), axis=0), down_weight).astype(jnp.bfloat16)
    reduced = lax.map(second_section, frame_index)
    out_average, out_inv = clip_moments(reduced, clip_id, GROUPS)
    return lax.map(lambda item: normalize(item[0], item[1], item[2], out_gain, out_shift).astype(jnp.bfloat16), (reduced, out_average, out_inv))
```

```python
import functools
import jax
import jax.numpy as jnp
from jax import lax
from jax.experimental import pallas as pl
from jax.experimental.pallas import tpu as pltpu
from jax.sharding import PartitionSpec as P

GROUPS = 32
EPS = 1e-06
F32 = jnp.float32
BF16 = jnp.bfloat16
HIGHEST = lax.Precision.HIGHEST
VMEM_LIMIT = 56 * 1024 * 1024
VMEM = pl.BlockSpec(memory_space=pltpu.VMEM)
SMEM = pl.BlockSpec(memory_space=pltpu.SMEM)


def iota(shape, dim):
    return lax.broadcasted_iota(jnp.int32, shape, dim)


def pack_row(sums, channels):
    size = channels // GROUPS
    gather = (iota((channels, 128), 0) // size == iota((channels, 128), 1) % GROUPS).astype(F32)
    stacked = jnp.concatenate(sums + [jnp.zeros((4, channels), F32)], axis=0)
    grouped = jnp.dot(stacked, gather, precision=HIGHEST, preferred_element_type=F32)
    place = iota((8, 128), 1) // GROUPS == iota((8, 128), 0)
    return jnp.sum(jnp.where(place, grouped, 0.0), axis=0, keepdims=True)


def clip_range(clip_ref, frame):
    mine = clip_ref[frame]
    begin, end = jnp.int32(0), jnp.int32(0)
    for t in range(clip_ref.shape[0]):
        other = clip_ref[t]
        begin = begin + (other < mine).astype(jnp.int32)
        end = end + (other <= mine).astype(jnp.int32)
    return begin, end


def scale_and_shift(rows, ranges, gain, offset, channels, cells, bands):
    size = channels // GROUPS
    frame = 2 * (iota(rows.shape, 0) // bands) + iota(rows.shape, 1) // 64
    lane, channel = iota((128, channels), 0), iota((128, channels), 1)
    to_sum = (lane % 64 == channel // size).astype(F32)
    to_square = (lane % 64 == GROUPS + channel // size).astype(F32)
    totals = [
        jnp.sum(jnp.where((frame >= b) & (frame < e), rows, 0.0), axis=0, keepdims=True)
        for b, e in ranges
    ]
    totals = jnp.concatenate(totals + [jnp.zeros((8 - len(ranges), 128), F32)], axis=0)
    sums = jnp.dot(totals, to_sum, precision=HIGHEST, preferred_element_type=F32)
    squares = jnp.dot(totals, to_square, precision=HIGHEST, preferred_element_type=F32)
    found = []
    for n, (b, e) in enumerate(ranges):
        count = (e - b).astype(F32) * cells
        mean = sums[n : n + 1] / count
        inv_std = lax.rsqrt(squares[n : n + 1] / count - mean * mean + EPS)
        scale = inv_std * gain
        found.append((scale, offset - mean * scale))
    return found


def sums_kernel(x_ref, row_ref, top_ref, bottom_ref):
    frames, rows, cols, channels = x_ref.shape
    sums = []
    for f in range(frames):
        one = jnp.zeros((8, channels), F32)
        two = jnp.zeros((8, channels), F32)
        for r in range(rows):
            v = x_ref[f, r].astype(F32).reshape(cols // 8, 8, channels)
            one = one + jnp.sum(v, axis=0)
            two = two + jnp.sum(v * v, axis=0)
        sums += [jnp.sum(one, axis=0, keepdims=True), jnp.sum(two, axis=0, keepdims=True)]
    row_ref[...] = jnp.broadcast_to(pack_row(sums, channels)[None], row_ref.shape)
    top_ref[...] = x_ref[:, 0:2]
    bottom_ref[...] = x_ref[:, rows - 1 : rows]


def conv_kernel(
    bands, cells,
    clip_ref, rows_ref, x_ref, before_ref, above_ref, above_before_ref, below_ref, below_before_ref,
    weight_ref, bias_ref, gain_ref, offset_ref, down_ref,
    residual_ref, partial_ref,
    hidden, own, weights, spread,
):
    frames, rows, cols, channels = x_ref.shape
    half = cols // 2
    first = lax.axis_index("tm") * frames
    band = lax.axis_index("band")
    ranges = [clip_range(clip_ref, first), clip_range(clip_ref, first + 1)]
    stats = scale_and_shift(
        rows_ref[...], ranges, gain_ref[...], offset_ref[...], channels, cells, bands
    )
    stats = [(0.5 * scale, 0.5 * shift) for scale, shift in stats]

    zero = jnp.zeros((channels, channels), BF16)
    for tap in range(9):
        w0, w1, w2 = (weight_ref[tap * 3 + dx] for dx in range(3))
        at = tap * 2 * channels
        weights[at : at + channels, :] = jnp.concatenate([w1, w0, zero, w2], axis=1)
        weights[at + channels : at + 2 * channels, :] = jnp.concatenate([w2, w1, w0, zero], axis=1)

    def split_row(value, slot):
        spread[slot] = value.astype(F32)
        return spread[slot, pl.ds(0, half, 2), :], spread[slot, pl.ds(1, half, 2), :]

    def put_row(value, slot, frame, row, keep, is_own):
        scale, shift = stats[1 if frame == 3 else 0]
        parts = split_row(value, slot)
        for side, part in enumerate(parts):
            lanes = pl.ds(side * channels, channels)
            if is_own:
                own[frame - 2, row - 1, :, lanes] = part.astype(BF16)
            u = part * scale + shift
            h = u + u * jnp.tanh(u)
            if keep is not None:
                h = h * keep
            hidden[frame, row, :, lanes] = h.astype(BF16)

    keep_above = (band > 0).astype(F32)
    keep_below = (band < bands - 1).astype(F32)
    for frame in range(4):
        f = frame % 2
        body, above, below = (
            (before_ref, above_before_ref, below_before_ref)
            if frame < 2
            else (x_ref, above_ref, below_ref)
        )
        put_row(above[f, 0], 0, frame, 0, keep_above, False)
        put_row(below[f, 0], 1, frame, rows + 1, keep_below, frame >= 2)
        put_row(below[f, 1], 2, frame, rows + 2, keep_below, False)

        @pl.loop(0, rows, unroll=2)
        def _(r):
            put_row(body[f, r], 3 + r % 2, frame, r + 1, None, frame >= 2)

    bias = jnp.concatenate([bias_ref[...]] * 2, axis=1)
    column = iota((half, channels), 0)
    for f in range(frames):
        begin = ranges[f][0]
        sources = [jnp.maximum(first + f - 2 + k, begin) - (first - 2) for k in range(3)]

        @pl.loop(0, rows + 1)
        def _(r):
            window = jnp.concatenate(
                [hidden[sources[k], r + dy] for k in range(3) for dy in range(3)], axis=1
            )
            found = jnp.dot(window, weights[...], preferred_element_type=F32)
            left = found[:, 2 * channels : 3 * channels]
            right = found[:, 3 * channels :]
            left = jnp.where(column == 0, 0.0, pltpu.roll(left, 1, 0))
            right = jnp.where(column == half - 1, 0.0, pltpu.roll(right, half - 1, 0))
            total = found[:, : 2 * channels] + jnp.concatenate([left, right], axis=1)
            total = total + own[f, r].astype(F32) + bias
            keep = jnp.where(r == rows, keep_below, 1.0)
            residual_ref[f, r] = (total * keep).astype(BF16)

    last = clip_ref.shape[0] - 1
    after = [clip_range(clip_ref, jnp.minimum(first + 2 + n, last))[0] for n in range(2)]
    source = (after[0] > first).astype(jnp.int32)
    takes = [(after[n] <= first + 1).astype(F32) for n in range(2)]
    partial_ref[0] = (
        down(residual_ref, down_ref, ((source, 0), (1, 1)), rows) * takes[0]
    ).astype(BF16)
    partial_ref[1] = (down(residual_ref, down_ref, ((1, 0),), rows) * takes[1]).astype(BF16)


def down(residual_ref, down_ref, pairs, rows):
    half, wide = residual_ref.shape[2:]
    channels = wide // 2
    main, side, main_w, side_w = [], [], [], []
    for frame, k in pairs:
        for dy in range(3):
            lines = jnp.concatenate([residual_ref[frame, 2 * i + dy] for i in range(rows // 2)], axis=0)
            main.append(lines)
            side.append(lines[:, :channels])
            at = (k * 9 + dy * 3) * channels
            main_w.append(down_ref[at : at + wide])
            side_w.append(down_ref[at + wide : at + wide + channels])
    cat = jnp.concatenate
    total = jnp.dot(cat(main, axis=1), cat(main_w, axis=0), preferred_element_type=F32)
    shifted = jnp.dot(cat(side, axis=1), cat(side_w, axis=0), preferred_element_type=F32)
    size = total.shape[0]
    column = iota(shifted.shape, 0) % half
    shifted = jnp.where(column == half - 1, 0.0, pltpu.roll(shifted, size - 1, 0))
    return (total + shifted).reshape(rows // 2, half, -1)


def local_kernel(rows, clip_ref, residual_ref, down_ref, out_ref):
    first = lax.axis_index("tm") * 2
    begin = [clip_range(clip_ref, first + n)[0] for n in range(2)]
    out_ref[0] = down(residual_ref, down_ref, ((0, 2),), rows)
    out_ref[1] = down(
        residual_ref, down_ref, (((begin[1] > first).astype(jnp.int32), 1), (1, 2)), rows
    )

    @pl.when(begin[0] == first)
    def _():
        out_ref[0] += down(residual_ref, down_ref, ((0, 0), (0, 1)), rows)

    @pl.when(begin[1] >= first)
    def _():
        out_ref[1] += down(residual_ref, down_ref, ((begin[1] - first, 0),), rows)


def join_kernel(local_ref, partial_ref, reduced_ref, row_ref):
    frames, lines, half, channels = local_ref.shape
    sums = []
    for f in range(frames):
        one = jnp.zeros((8, channels), F32)
        two = jnp.zeros((8, channels), F32)
        for i in range(lines):
            v = (local_ref[f, i] + partial_ref[f, i].astype(F32)).astype(BF16)
            reduced_ref[f, i] = v
            v = v.astype(F32).reshape(half // 8, 8, channels)
            one = one + jnp.sum(v, axis=0)
            two = two + jnp.sum(v * v, axis=0)
        sums += [jnp.sum(one, axis=0, keepdims=True), jnp.sum(two, axis=0, keepdims=True)]
    row_ref[...] = jnp.broadcast_to(pack_row(sums, channels)[None], row_ref.shape)


def out_kernel(bands, cells, clip_ref, rows_ref, reduced_ref, gain_ref, offset_ref, out_ref):
    frames, lines, half, channels = reduced_ref.shape
    first = lax.axis_index("tm") * frames
    ranges = [clip_range(clip_ref, first + n) for n in range(2)]
    stats = scale_and_shift(
        rows_ref[...], ranges, gain_ref[...], offset_ref[...], channels, cells, bands
    )
    for f in range(frames):
        scale, shift = stats[f]
        for i in range(lines):
            out_ref[f, i] = (reduced_ref[f, i].astype(F32) * scale + shift).astype(BF16)


def call(kernel, out_shape, in_specs, scratch=(), flops=0, moved=0):
    return pl.pallas_call(
        kernel,
        out_shape=out_shape,
        in_specs=in_specs,
        out_specs=jax.tree.map(lambda _: VMEM, out_shape),
        scratch_shapes=list(scratch),
        compiler_params=pltpu.CompilerParams(vmem_limit_bytes=VMEM_LIMIT),
        cost_estimate=pl.CostEstimate(flops=flops, bytes_accessed=moved, transcendentals=0),
    )


def shifted(array, tm_by, band_by):
    tms, bands = lax.axis_size("tm"), lax.axis_size("band")
    pairs = []
    for i in range(tms):
        for b in range(bands):
            if 0 <= i + tm_by < tms and 0 <= b + band_by < bands:
                pairs.append((i * bands + b, (i + tm_by) * bands + b + band_by))
    return lax.ppermute(array, ("tm", "band"), pairs)


def on_device(
    frames_in, clip_id, conv_weight, conv_bias, norm_gain, norm_shift, down_weight, out_gain, out_shift
):
    frames, rows, cols, channels = frames_in.shape
    wide = down_weight.shape[-1]
    tms, bands = lax.axis_size("tm"), lax.axis_size("band")
    devices, half, lines = tms * bands, cols // 2, rows // 2
    shape = jax.ShapeDtypeStruct
    everyone = shape((devices, 1, 128), F32)

    def exchange(row):
        return lax.all_to_all(row, ("tm", "band"), 0, 0, tiled=True).reshape(devices, 128)

    before = shifted(frames_in, 1, 0)
    row, top, bottom = call(
        sums_kernel,
        (everyone, shape((frames, 2, cols, channels), BF16), shape((frames, 1, cols, channels), BF16)),
        [VMEM],
        moved=1 << 20,
    )(frames_in)
    above, above_before = shifted(bottom, 0, 1), shifted(bottom, 1, 1)
    below, below_before = shifted(top, 0, -1), shifted(top, 1, -1)
    sums = exchange(row)
    residual, partial = call(
        functools.partial(conv_kernel, bands, float(bands * rows * cols * (channels // GROUPS))),
        (shape((frames, rows + 1, half, 2 * channels), BF16), shape((frames, lines, half, wide), BF16)),
        [SMEM] + [VMEM] * 12,
        scratch=[
            pltpu.VMEM((4, rows + 3, half, 2 * channels), BF16),
            pltpu.VMEM((frames, rows + 1, half, 2 * channels), BF16),
            pltpu.VMEM((18 * channels, 4 * channels), BF16),
            pltpu.VMEM((5, cols, channels), F32),
        ],
        flops=1 << 32,
        moved=1 << 23,
    )(
        clip_id, sums, frames_in, before, above, above_before, below, below_before,
        conv_weight.reshape(27, channels, channels), conv_bias.reshape(1, -1),
        norm_gain.reshape(1, -1), norm_shift.reshape(1, -1), down_weight.reshape(-1, wide),
    )
    arrived = shifted(partial, 1, 0)
    local = call(
        functools.partial(local_kernel, rows),
        shape((frames, lines, half, wide), F32),
        [SMEM, VMEM, VMEM],
        flops=1 << 31,
        moved=1 << 22,
    )(clip_id, residual, down_weight.reshape(-1, wide))
    reduced, row = call(
        join_kernel,
        (shape((frames, lines, half, wide), BF16), everyone),
        [VMEM, VMEM],
        moved=1 << 21,
    )(local, arrived)
    sums = exchange(row)
    return call(
        functools.partial(out_kernel, bands, float(bands * lines * half * (wide // GROUPS))),
        shape((frames, lines, half, wide), BF16),
        [SMEM] + [VMEM] * 4,
        moved=1 << 20,
    )(clip_id, sums, reduced, out_gain.reshape(1, -1), out_shift.reshape(1, -1))


def solution(mesh):
    return jax.shard_map(
        on_device,
        mesh=mesh,
        in_specs=(P("tm", "band", None, None), P(), P(), P(), P(), P(), P(), P(), P()),
        out_specs=P("tm", "band", None, None),
        check_vma=False,
    )
```

```python
import functools
import jax
import jax.numpy as jnp
from jax import lax
from jax.experimental import pallas as pl
from jax.experimental.pallas import tpu as pltpu
from jax.sharding import PartitionSpec as P

GROUPS = 32
EPS = 1e-06
F32 = jnp.float32
BF16 = jnp.bfloat16
VMEM = pl.BlockSpec(memory_space=pltpu.VMEM)
cat = jnp.concatenate


def iota(shape, dim):
    return lax.broadcasted_iota(jnp.int32, shape, dim)


def exact_dot(rows, zero_one):
    n = rows.shape[0]
    high = rows.astype(BF16)
    rest = rows - high.astype(F32)
    middle = rest.astype(BF16)
    low = (rest - middle.astype(F32)).astype(BF16)
    parts = cat([high.astype(F32), middle.astype(F32), low.astype(F32)], axis=0)
    spare = -parts.shape[0] % 16
    if spare:
        parts = cat([parts, jnp.zeros((spare, parts.shape[1]), F32)], axis=0)
    found = jnp.dot(parts.astype(BF16), zero_one.astype(BF16), preferred_element_type=F32)
    return found[:n] + found[n : 2 * n] + found[2 * n : 3 * n]


def pack_row(sums):
    channels = sums[0].shape[1]
    size = channels // GROUPS
    gather = iota((channels, 128), 0) // size == iota((channels, 128), 1) % GROUPS
    grouped = exact_dot(cat(sums, axis=0), gather.astype(F32))
    place = iota((4, 128), 1) // GROUPS == iota((4, 128), 0)
    return jnp.sum(jnp.where(place, grouped, 0.0), axis=0, keepdims=True)


def frame_sums(lines):
    deep = 64
    channels = lines[0].shape[1]
    one, two = jnp.zeros((deep, channels), F32), jnp.zeros((deep, channels), F32)
    for v in lines:
        for a in range(0, v.shape[0], deep):
            part = v[a : a + deep]
            one, two = one + part, two + part * part
    return [jnp.sum(one, axis=0, keepdims=True), jnp.sum(two, axis=0, keepdims=True)]


def scale_and_shift(rows, info_ref, gain, offset, cells, bands):
    channels = gain.shape[1]
    size = channels // GROUPS
    frame = 2 * (iota(rows.shape, 0) // bands) + iota(rows.shape, 1) // 64
    lane, channel = iota((128, 2 * channels), 0) % 64, iota((128, 2 * channels), 1)
    spread = lane == GROUPS * (channel // channels) + channel % channels // size
    totals = []
    for n in range(2):
        begin, end = info_ref[n : n + 1, :], info_ref[4 + n : 5 + n, :]
        inside = jnp.where((frame >= begin) & (frame < end), rows, 0.0)
        totals.append(jnp.sum(inside, axis=0, keepdims=True))
    sums = exact_dot(cat(totals, axis=0), spread.astype(F32))
    found = []
    for n in range(2):
        frames = (info_ref[4 + n : 5 + n, :] - info_ref[n : n + 1, :]).astype(F32)
        per = 1.0 / (cat([frames] * (channels // 128), axis=1) * cells)
        mean = sums[n : n + 1, :channels] * per
        inv_std = lax.rsqrt(sums[n : n + 1, channels:] * per - mean * mean + EPS)
        scale = inv_std * gain
        found.append((scale, offset - mean * scale))
    return found


def sums_kernel(x_ref, row_ref):
    sums = []
    for f in range(x_ref.shape[0]):
        sums += frame_sums([x_ref[f, r].astype(F32) for r in range(x_ref.shape[1])])
    row_ref[...] = jnp.broadcast_to(pack_row(sums)[None], row_ref.shape)


def setup_kernel(
    clip_ref, weight_ref, bias_ref, gain_ref, offset_ref, out_gain_ref, out_offset_ref,
    weights_ref, info_ref, vectors_ref,
):
    channels = bias_ref.shape[1]
    zero = jnp.zeros((channels, channels), BF16)
    for tap in range(9):
        w0, w1, w2 = (weight_ref[tap, dx] for dx in range(3))
        weights_ref[tap, 0:channels] = cat([w1, w0, zero, w2], axis=1)
        weights_ref[tap, channels : 2 * channels] = cat([w2, w1, w0, zero], axis=1)
    ids = clip_ref[...].astype(F32)
    lane = iota(ids.shape, 1)
    first = lax.axis_index("tm") * 2
    begins, ends = [], []
    for n in range(4):
        at = jnp.minimum(first + n, ids.shape[1] - 1)
        mine = jnp.sum(jnp.where(lane == at, ids, 0.0), axis=1, keepdims=True)
        begins.append(jnp.sum(jnp.where(ids < mine, 1.0, 0.0), axis=1, keepdims=True))
        ends.append(jnp.sum(jnp.where(ids <= mine, 1.0, 0.0), axis=1, keepdims=True))
    table = cat([jnp.broadcast_to(v, (1, 128)) for v in begins + ends], axis=0)
    info_ref[...] = table.astype(jnp.int32)
    blank = jnp.zeros((1, channels), F32)
    vectors_ref[...] = cat(
        [cat([ref[...], blank], axis=1) for ref in (bias_ref, gain_ref, offset_ref)]
        + [out_gain_ref[...], out_offset_ref[...], jnp.zeros((3, 2 * channels), F32)],
        axis=0,
    )


def edges_kernel(before_ref, x_ref, top_ref, bottom_ref):
    rows = x_ref.shape[1]
    for f in range(4):
        source = before_ref if f < 2 else x_ref
        top_ref[f] = source[f % 2, 0:2]
        bottom_ref[f, 0] = source[f % 2, rows - 1]


def activate(value, slot, scale, shift, hidden_at, own_at=None, keep=None):
    cols, channels = value.shape
    slot[...] = value.astype(F32)
    for side in range(2):
        lanes = pl.ds(side * channels, channels)
        part = slot[pl.ds(side, cols // 2, 2), :]
        if own_at is not None:
            own_at[:, lanes] = part.astype(BF16)
        u = part * scale + shift
        h = u + u * jnp.tanh(u)
        if keep is not None:
            h = h * keep
        hidden_at[:, lanes] = h.astype(BF16)


def convolve(line, weights_ref, outputs):
    weights = weights_ref[...].reshape(-1, weights_ref.shape[2])
    window = cat(
        [
            cat([line(sources[k], r + dy) for sources, r in outputs], axis=0)
            for k in range(3)
            for dy in (-1, 0, 1)
        ],
        axis=1,
    )
    found = jnp.dot(window, weights, preferred_element_type=F32)
    wide = found.shape[1] // 2
    channels = wide // 2
    size = found.shape[0]
    half = size // len(outputs)
    column = iota((size, channels), 0) % half
    from_left = jnp.where(column == 0, 0.0, pltpu.roll(found[:, wide : wide + channels], 1, 0))
    from_right = jnp.where(column == half - 1, 0.0, pltpu.roll(found[:, wide + channels :], size - 1, 0))
    total = found[:, :wide] + cat([from_left, from_right], axis=1)
    return [total[n * half : (n + 1) * half] for n in range(len(outputs))]


def strided(lines, down_ref, k):
    wide = down_ref.shape[1]
    channels = down_ref.shape[0] // 27
    windows = [lines(dy) for dy in range(3)]
    half = windows[0].shape[1]
    windows = [w.reshape(-1, wide) for w in windows]
    places = [(k * 9 + dy * 3) * channels for dy in range(3)]
    both = cat([down_ref[at : at + 2 * channels] for at in places], axis=0)
    next_even = cat([down_ref[at + 2 * channels : at + 3 * channels] for at in places], axis=0)
    total = jnp.dot(cat(windows, axis=1), both, preferred_element_type=F32)
    shifted = jnp.dot(
        cat([w[:, :channels] for w in windows], axis=1), next_even, preferred_element_type=F32
    )
    size = total.shape[0]
    column = iota(shifted.shape, 0) % half
    shifted = jnp.where(column == half - 1, 0.0, pltpu.roll(shifted, size - 1, 0))
    return (total + shifted).reshape(-1, half, wide)


def hand_on(line, outputs, info_ref, first, down_ref, partial_ref):
    begins = [info_ref[2, 0], info_ref[3, 0]]
    source = (begins[0] > first).astype(jnp.int32)
    takes = [(b <= first + 1).astype(F32) for b in begins]

    def both(dy):
        return jnp.stack([line(f, 2 * i + dy) for f in (source, 1) for i in outputs])

    def second(dy):
        return jnp.stack([line(1, 2 * i + dy) for i in outputs])

    n = len(outputs)
    older = strided(both, down_ref, 0)
    newer = strided(second, down_ref, 1)
    partial_ref[0] = ((older[:n] + newer) * takes[0]).astype(BF16)
    partial_ref[1] = (older[n:] * takes[1]).astype(BF16)


def frame_sources(info_ref, first):
    return [
        [jnp.maximum(first + f - 2 + k, info_ref[f, 0]) - (first - 2) for k in range(3)] for f in range(2)
    ]


def inner_kernel(
    bands, cells, rows_ref, info_ref, vectors_ref, x_ref, before_ref, weights_ref, down_ref,
    hidden_ref, stats_ref, residual_ref, partial_ref, own, slots,
):
    frames, rows, cols, channels = x_ref.shape
    first = lax.axis_index("tm") * frames
    bias, gain, offset = (vectors_ref[n : n + 1, :channels] for n in range(3))
    stats = scale_and_shift(rows_ref[...], info_ref, gain, offset, cells, bands)
    stats = [(0.5 * scale, 0.5 * shift) for scale, shift in stats]
    stats_ref[...] = cat([v for pair in stats for v in pair] + [jnp.zeros((4, channels), F32)], axis=0)
    for frame in range(4):
        scale, shift = stats[1 if frame == 3 else 0]
        for r in range(rows):
            activate(
                (before_ref if frame < 2 else x_ref)[frame % 2, r],
                slots.at[r],
                scale,
                shift,
                hidden_ref.at[frame, r],
                own.at[frame - 2, r - 1] if frame >= 2 and 0 < r < rows - 1 else None,
            )
    sources = frame_sources(info_ref, first)
    outputs = [(f, r) for f in range(frames) for r in range(1, rows - 1)]
    found = convolve(
        lambda source, r: hidden_ref[source, r], weights_ref, [(sources[f], r) for f, r in outputs]
    )
    bias = cat([bias, bias], axis=1)
    for (f, r), total in zip(outputs, found):
        residual_ref[f, r - 1] = (total + own[f, r - 1].astype(F32) + bias).astype(BF16)
    hand_on(lambda f, r: residual_ref[f, r - 1], (1, 2), info_ref, first, down_ref, partial_ref)


def edge_kernel(
    bands, info_ref, vectors_ref, stats_ref, x_ref, hidden_ref, above_ref, below_ref, inner_ref,
    weights_ref, down_ref, residual_ref, partial_ref, rim, own, slots,
):
    frames, rows, cols, channels = x_ref.shape
    first = lax.axis_index("tm") * frames
    band = lax.axis_index("band")
    keep_above = (band > 0).astype(F32)
    keep_below = (band < bands - 1).astype(F32)
    for frame in range(4):
        n = 2 if frame == 3 else 0
        scale, shift = stats_ref[n : n + 1, :], stats_ref[n + 1 : n + 2, :]
        owned = own.at[frame - 2, 2] if frame >= 2 else None
        activate(above_ref[frame, 0], slots.at[0], scale, shift, rim.at[frame, 0], None, keep_above)
        activate(below_ref[frame, 0], slots.at[1], scale, shift, rim.at[frame, 1], owned, keep_below)
        activate(below_ref[frame, 1], slots.at[2], scale, shift, rim.at[frame, 2], None, keep_below)
    for f in range(frames):
        for n, r in enumerate((0, rows - 1)):
            slots[3 + n] = x_ref[f, r].astype(F32)
            for side in range(2):
                own[f, n, :, pl.ds(side * channels, channels)] = slots[
                    3 + n, pl.ds(side, cols // 2, 2), :
                ].astype(BF16)

    def line(source, r):
        if r < 0:
            return rim[source, 0]
        return hidden_ref[source, r] if r < rows else rim[source, 1 + r - rows]

    sources = frame_sources(info_ref, first)
    outputs = [(f, r) for f in range(frames) for r in (0, rows - 1, rows)]
    found = convolve(line, weights_ref, [(sources[f], r) for f, r in outputs])
    bias = vectors_ref[0:1, :channels]
    bias = cat([bias, bias], axis=1)
    for n, total in enumerate(found):
        f, place = n // 3, n % 3
        value = total + own[f, place].astype(F32) + bias
        if place == 2:
            value = value * keep_below
        residual_ref[f, place] = value.astype(BF16)
    hand_on(
        lambda f, r: residual_line(inner_ref, residual_ref, rows, f, r),
        (0, rows // 2 - 1), info_ref, first, down_ref, partial_ref,
    )


def residual_line(inner_ref, edge_ref, rows, f, r):
    if 0 < r < rows - 1:
        return inner_ref[f, r - 1]
    return edge_ref[f, 0 if r == 0 else r - rows + 2]


def local_kernel(rows, info_ref, inner_ref, edge_ref, down_ref, out_ref):
    first = lax.axis_index("tm") * 2
    begins = [info_ref[0, 0], info_ref[1, 0]]

    def lines(*picked):
        return lambda dy: jnp.stack(
            [residual_line(inner_ref, edge_ref, rows, f, 2 * i + dy) for f in picked for i in range(rows // 2)]
        )

    base = strided(lines(0, 1), down_ref, 2)
    out_ref[0] = base[: rows // 2]
    out_ref[1] = base[rows // 2 :] + strided(lines((begins[1] > first).astype(jnp.int32)), down_ref, 1)

    @pl.when(begins[0] == first)
    def _():
        out_ref[0] += strided(lines(0), down_ref, 0) + strided(lines(0), down_ref, 1)

    @pl.when(begins[1] >= first)
    def _():
        out_ref[1] += strided(lines(begins[1] - first), down_ref, 0)


def join_kernel(local_ref, inner_ref, edge_ref, reduced_ref, row_ref):
    frames, lines, half, channels = local_ref.shape
    sums = []
    for f in range(frames):
        values = []
        for i in range(lines):
            sent = inner_ref[f, i - 1] if 0 < i < lines - 1 else edge_ref[f, min(i, 1)]
            v = (local_ref[f, i] + sent.astype(F32)).astype(BF16)
            reduced_ref[f, i] = v
            values.append(v.astype(F32))
        sums += frame_sums(values)
    row_ref[...] = jnp.broadcast_to(pack_row(sums)[None], row_ref.shape)


def out_kernel(bands, cells, rows_ref, info_ref, vectors_ref, reduced_ref, out_ref):
    frames, lines = reduced_ref.shape[:2]
    stats = scale_and_shift(
        rows_ref[...], info_ref, vectors_ref[3:4, :], vectors_ref[4:5, :], cells, bands
    )
    for f in range(frames):
        scale, shift = stats[f]
        for i in range(lines):
            out_ref[f, i] = (reduced_ref[f, i].astype(F32) * scale + shift).astype(BF16)


def call(kernel, out_shape, in_specs, scratch=(), megabytes=4, flops=0, moved=0):
    return pl.pallas_call(
        kernel,
        out_shape=out_shape,
        in_specs=in_specs,
        out_specs=jax.tree.map(lambda _: VMEM, out_shape),
        scratch_shapes=list(scratch),
        compiler_params=pltpu.CompilerParams(vmem_limit_bytes=megabytes << 20),
        cost_estimate=pl.CostEstimate(flops=flops, bytes_accessed=moved, transcendentals=0),
    )


def passed_on(array, axis, by):
    peers = lax.axis_size(axis)
    pairs = [(i, i + by) for i in range(peers) if 0 <= i + by < peers]
    return lax.ppermute(array, axis, pairs)


def on_device(
    frames_in, clip_id, conv_weight, conv_bias, norm_gain, norm_shift, down_weight, out_gain, out_shift
):
    frames, rows, cols, channels = frames_in.shape
    wide = down_weight.shape[-1]
    bands = lax.axis_size("band")
    devices, half, lines = lax.axis_size("tm") * bands, cols // 2, rows // 2
    shape = jax.ShapeDtypeStruct
    everyone = shape((devices, 1, 128), F32)

    def exchange(row):
        return lax.all_to_all(row, ("tm", "band"), 0, 0, tiled=True).reshape(devices, 128)

    before = passed_on(frames_in, "tm", 1)
    row = call(sums_kernel, everyone, [VMEM], flops=1 << 33, moved=1 << 20)(frames_in)
    weights, info, vectors = call(
        setup_kernel,
        (
            shape((9, 2 * channels, 4 * channels), BF16),
            shape((8, 128), jnp.int32),
            shape((8, wide), F32),
        ),
        [VMEM] * 7,
        megabytes=8,
        flops=1 << 32,
        moved=1 << 22,
    )(
        clip_id.reshape(1, -1), conv_weight.reshape(9, 3, channels, channels), conv_bias.reshape(1, -1),
        norm_gain.reshape(1, -1), norm_shift.reshape(1, -1), out_gain.reshape(1, -1), out_shift.reshape(1, -1),
    )
    down = down_weight.reshape(-1, wide)
    sums = exchange(row)
    top, bottom = call(
        edges_kernel,
        (shape((4, 2, cols, channels), BF16), shape((4, 1, cols, channels), BF16)),
        [VMEM] * 2,
        flops=1 << 33,
        moved=1 << 20,
        megabytes=8,
    )(before, frames_in)
    below, above = passed_on(top, "band", -1), passed_on(bottom, "band", 1)
    hidden, stats, inner, inner_partial = call(
        functools.partial(inner_kernel, bands, float(bands * rows * cols * (channels // GROUPS))),
        (
            shape((4, rows, half, 2 * channels), BF16),
            shape((8, channels), F32),
            shape((frames, rows - 2, half, 2 * channels), BF16),
            shape((frames, lines - 2, half, wide), BF16),
        ),
        [VMEM] * 7,
        scratch=[
            pltpu.VMEM((frames, rows - 2, half, 2 * channels), BF16),
            pltpu.VMEM((rows, cols, channels), F32),
        ],
        megabytes=24,
        flops=5 << 30,
        moved=1 << 23,
    )(sums, info, vectors, frames_in, before, weights, down)
    inner_arrived = passed_on(inner_partial, "tm", 1)
    edge, edge_partial = call(
        functools.partial(edge_kernel, bands),
        (
            shape((frames, 3, half, 2 * channels), BF16),
            shape((frames, 2, half, wide), BF16),
        ),
        [VMEM] * 10,
        scratch=[
            pltpu.VMEM((4, 3, half, 2 * channels), BF16),
            pltpu.VMEM((frames, 3, half, 2 * channels), BF16),
            pltpu.VMEM((5, cols, channels), F32),
        ],
        megabytes=24,
        flops=2 << 30,
        moved=1 << 22,
    )(info, vectors, stats, frames_in, hidden, above, below, inner, weights, down)
    edge_arrived = passed_on(edge_partial, "tm", 1)
    local = call(
        functools.partial(local_kernel, rows),
        shape((frames, lines, half, wide), F32),
        [VMEM] * 4,
        megabytes=16,
        flops=1 << 31,
        moved=1 << 22,
    )(info, inner, edge, down)
    reduced, row = call(
        join_kernel,
        (shape((frames, lines, half, wide), BF16), everyone),
        [VMEM] * 3,
        megabytes=8,
        moved=1 << 21,
    )(local, inner_arrived, edge_arrived)
    return call(
        functools.partial(out_kernel, bands, float(bands * lines * half * (wide // GROUPS))),
        shape((frames, lines, half, wide), BF16),
        [VMEM] * 4,
        megabytes=8,
        moved=1 << 20,
    )(exchange(row), info, vectors, reduced)


def solution(mesh):
    return jax.shard_map(
        on_device,
        mesh=mesh,
        in_specs=(P("tm", "band", None, None), P(), P(), P(), P(), P(), P(), P(), P()),
        out_specs=P("tm", "band", None, None),
        check_vma=False,
    )
```

```python
import functools
import jax
import jax.numpy as jnp
from jax import lax
from jax.experimental import pallas as pl
from jax.experimental.pallas import tpu as pltpu
from jax.sharding import PartitionSpec as P

GROUPS = 32
EPS = 1e-06
F32 = jnp.float32
BF16 = jnp.bfloat16
VMEM = pl.BlockSpec(memory_space=pltpu.VMEM)
cat = jnp.concatenate


def iota(shape, dim):
    return lax.broadcasted_iota(jnp.int32, shape, dim)


def exact_dot(rows, zero_one):
    n = rows.shape[0]
    high = rows.astype(BF16)
    rest = rows - high.astype(F32)
    middle = rest.astype(BF16)
    low = (rest - middle.astype(F32)).astype(BF16)
    parts = cat([high.astype(F32), middle.astype(F32), low.astype(F32)], axis=0)
    spare = -parts.shape[0] % 16
    if spare:
        parts = cat([parts, jnp.zeros((spare, parts.shape[1]), F32)], axis=0)
    found = jnp.dot(parts.astype(BF16), zero_one.astype(BF16), preferred_element_type=F32)
    return found[:n] + found[n : 2 * n] + found[2 * n : 3 * n]


def pack_row(sums):
    channels = sums[0].shape[1]
    size = channels // GROUPS
    gather = iota((channels, 128), 0) // size == iota((channels, 128), 1) % GROUPS
    grouped = exact_dot(cat(sums, axis=0), gather.astype(F32))
    place = iota((4, 128), 1) // GROUPS == iota((4, 128), 0)
    return jnp.sum(jnp.where(place, grouped, 0.0), axis=0, keepdims=True)


def frame_sums(lines):
    deep = 64
    channels = lines[0].shape[1]
    one, two = jnp.zeros((deep, channels), F32), jnp.zeros((deep, channels), F32)
    for v in lines:
        for a in range(0, v.shape[0], deep):
            part = v[a : a + deep]
            one, two = one + part, two + part * part
    return [jnp.sum(one, axis=0, keepdims=True), jnp.sum(two, axis=0, keepdims=True)]


def scale_and_shift(rows, info_ref, gain, offset, cells, bands):
    channels = gain.shape[1]
    size = channels // GROUPS
    frame = 2 * (iota(rows.shape, 0) // bands) + iota(rows.shape, 1) // 64
    lane, channel = iota((128, 2 * channels), 0) % 64, iota((128, 2 * channels), 1)
    spread = lane == GROUPS * (channel // channels) + channel % channels // size
    totals = []
    for n in range(2):
        begin, end = info_ref[n : n + 1, :], info_ref[4 + n : 5 + n, :]
        inside = jnp.where((frame >= begin) & (frame < end), rows, 0.0)
        totals.append(jnp.sum(inside, axis=0, keepdims=True))
    sums = exact_dot(cat(totals, axis=0), spread.astype(F32))
    found = []
    for n in range(2):
        frames = (info_ref[4 + n : 5 + n, :] - info_ref[n : n + 1, :]).astype(F32)
        per = 1.0 / (cat([frames] * (channels // 128), axis=1) * cells)
        mean = sums[n : n + 1, :channels] * per
        inv_std = lax.rsqrt(sums[n : n + 1, channels:] * per - mean * mean + EPS)
        scale = inv_std * gain
        found.append((scale, offset - mean * scale))
    return found


def sums_kernel(x_ref, row_ref, top_ref, bottom_ref):
    frames, rows = x_ref.shape[:2]
    top_ref[...] = x_ref[:, 0:2]
    bottom_ref[...] = x_ref[:, rows - 1 : rows]
    sums = []
    for f in range(frames):
        sums += frame_sums([x_ref[f, r].astype(F32) for r in range(rows)])
    row_ref[...] = jnp.broadcast_to(pack_row(sums)[None], row_ref.shape)


def arrange(weight_ref, weights):
    channels = weight_ref.shape[2]
    zero = jnp.zeros((channels, channels), BF16)
    for tap in range(9):
        w0, w1, w2 = (weight_ref[tap, dx] for dx in range(3))
        weights[tap, 0:channels] = cat([w1, w0, zero, w2], axis=1)
        weights[tap, channels : 2 * channels] = cat([w2, w1, w0, zero], axis=1)


def clip_table(clip_ref, first):
    ids = clip_ref[...].astype(F32)
    lane = iota(ids.shape, 1)
    begins, ends = [], []
    for n in range(4):
        at = jnp.minimum(first + n, ids.shape[1] - 1)
        mine = jnp.sum(jnp.where(lane == at, ids, 0.0), axis=1, keepdims=True)
        begins.append(jnp.sum(jnp.where(ids < mine, 1.0, 0.0), axis=1, keepdims=True))
        ends.append(jnp.sum(jnp.where(ids <= mine, 1.0, 0.0), axis=1, keepdims=True))
    return cat([jnp.broadcast_to(v, (1, 128)) for v in begins + ends], axis=0).astype(jnp.int32)


def activated(value, scale, shift):
    u = value.astype(F32) * scale + shift
    return u + u * jnp.tanh(u)


def convolve(line, weights_ref, outputs):
    weights = weights_ref[...].reshape(-1, weights_ref.shape[2])
    window = cat(
        [
            cat([line(sources[k], r + dy) for sources, r in outputs], axis=0)
            for k in range(3)
            for dy in (-1, 0, 1)
        ],
        axis=1,
    )
    found = jnp.dot(window, weights, preferred_element_type=F32)
    wide = found.shape[1] // 2
    channels = wide // 2
    size = found.shape[0]
    half = size // len(outputs)
    column = iota((size, channels), 0) % half
    from_left = jnp.where(column == 0, 0.0, pltpu.roll(found[:, wide : wide + channels], 1, 0))
    from_right = jnp.where(column == half - 1, 0.0, pltpu.roll(found[:, wide + channels :], size - 1, 0))
    total = found[:, :wide] + cat([from_left, from_right], axis=1)
    return [total[n * half : (n + 1) * half] for n in range(len(outputs))]


def strided(lines, down_ref, k):
    wide = down_ref.shape[1]
    channels = down_ref.shape[0] // 27
    windows = [lines(dy) for dy in range(3)]
    half = windows[0].shape[1]
    windows = [w.reshape(-1, wide) for w in windows]
    places = [(k * 9 + dy * 3) * channels for dy in range(3)]
    both = cat([down_ref[at : at + 2 * channels] for at in places], axis=0)
    next_even = cat([down_ref[at + 2 * channels : at + 3 * channels] for at in places], axis=0)
    total = jnp.dot(cat(windows, axis=1), both, preferred_element_type=F32)
    shifted = jnp.dot(
        cat([w[:, :channels] for w in windows], axis=1), next_even, preferred_element_type=F32
    )
    size = total.shape[0]
    column = iota(shifted.shape, 0) % half
    shifted = jnp.where(column == half - 1, 0.0, pltpu.roll(shifted, size - 1, 0))
    return (total + shifted).reshape(-1, half, wide)


def hand_on(line, outputs, info_ref, first, down_ref, partial_ref):
    begins = [info_ref[2, 0], info_ref[3, 0]]
    source = (begins[0] > first).astype(jnp.int32)
    goes = lax.axis_index("tm") < lax.axis_size("tm") - 1
    takes = [(goes & (b <= first + 1)).astype(F32) for b in begins]

    def both(dy):
        return jnp.stack([line(f, 2 * i + dy) for f in (source, 1) for i in outputs])

    def second(dy):
        return jnp.stack([line(1, 2 * i + dy) for i in outputs])

    n = len(outputs)
    older = strided(both, down_ref, 0)
    newer = strided(second, down_ref, 1)
    partial_ref[0] = ((older[:n] + newer) * takes[0]).astype(BF16)
    partial_ref[1] = (older[n:] * takes[1]).astype(BF16)


def frame_sources(info_ref, first):
    return [
        [jnp.maximum(first + f - 2 + k, info_ref[f, 0]) - (first - 2) for k in range(3)] for f in range(2)
    ]


def conv_kernel(
    bands, cells, rows_ref, clip_ref, bias_ref, gain_ref, offset_ref, weight_ref, down_ref,
    x_ref, before_ref, above_ref, above_before_ref, below_ref, below_before_ref,
    residual_ref, partial_ref, info_ref, hidden, own, weights, slots,
):
    rows, cols, channels = x_ref.shape[1:]
    first = lax.axis_index("tm") * 2
    band = lax.axis_index("band")
    keep_above = (band > 0).astype(F32)
    keep_below = (band < bands - 1).astype(F32)
    info_ref[...] = clip_table(clip_ref, first)
    arrange(weight_ref, weights)
    bias = bias_ref[...]
    stats = scale_and_shift(rows_ref[...], info_ref, gain_ref[...], offset_ref[...], cells, bands)
    stats = [0.5 * v for pair in stats for v in pair]
    for frame in range(4):
        scale, shift = stats[2:] if frame == 3 else stats[:2]
        body, above, below = (
            (before_ref, above_before_ref, below_before_ref)
            if frame < 2
            else (x_ref, above_ref, below_ref)
        )
        f = frame % 2
        lines = [above.at[f, 0]] + [body.at[f, r] for r in range(rows)] + [below.at[f, r] for r in range(2)]
        for n, line in enumerate(lines):
            slot = slots.at[n]
            slot[...] = line[...].astype(F32)
            for side in range(2):
                lanes = pl.ds(side * channels, channels)
                value = slot[pl.ds(side, cols // 2, 2), :]
                if frame >= 2 and 1 <= n < rows + 2:
                    own[f, n - 1, :, lanes] = value.astype(BF16)
                value = activated(value, scale, shift)
                if n == 0:
                    value = value * keep_above
                if n > rows:
                    value = value * keep_below
                hidden[frame, n, :, lanes] = value.astype(BF16)
    sources = frame_sources(info_ref, first)
    bias = cat([bias, bias], axis=1)
    for f in range(2):
        found = convolve(
            lambda source, r: hidden[source, r + 1], weights, [(sources[f], r) for r in range(rows + 1)]
        )
        for r, total in enumerate(found):
            value = total + own[f, r].astype(F32) + bias
            if r == rows:
                value = value * keep_below
            residual_ref[f, r] = value.astype(BF16)
    hand_on(
        lambda f, r: residual_ref[f, r], range(rows // 2), info_ref, first, down_ref, partial_ref
    )


def local_kernel(info_ref, residual_ref, down_ref, out_ref):
    first = lax.axis_index("tm") * 2
    begins = [info_ref[0, 0], info_ref[1, 0]]
    count = out_ref.shape[1]

    def lines(*picked):
        return lambda dy: jnp.stack([residual_ref[f, 2 * i + dy] for f in picked for i in range(count)])

    base = strided(lines(0, 1), down_ref, 2)
    out_ref[0] = base[:count]
    out_ref[1] = base[count:] + strided(lines((begins[1] > first).astype(jnp.int32)), down_ref, 1)

    @pl.when(begins[0] == first)
    def _():
        out_ref[0] += strided(lines(0), down_ref, 0) + strided(lines(0), down_ref, 1)

    @pl.when(begins[1] >= first)
    def _():
        out_ref[1] += strided(lines(begins[1] - first), down_ref, 0)


def join_kernel(local_ref, sent_ref, reduced_ref, row_ref):
    frames, lines, half, channels = local_ref.shape
    sums = []
    for f in range(frames):
        values = []
        for i in range(lines):
            v = (local_ref[f, i] + sent_ref[f, i].astype(F32)).astype(BF16)
            reduced_ref[f, i] = v
            values.append(v.astype(F32))
        sums += frame_sums(values)
    row_ref[...] = jnp.broadcast_to(pack_row(sums)[None], row_ref.shape)


def out_kernel(bands, cells, rows_ref, info_ref, gain_ref, offset_ref, reduced_ref, out_ref):
    frames, lines = reduced_ref.shape[:2]
    stats = scale_and_shift(rows_ref[...], info_ref, gain_ref[...], offset_ref[...], cells, bands)
    for f in range(frames):
        scale, shift = stats[f]
        for i in range(lines):
            out_ref[f, i] = (reduced_ref[f, i].astype(F32) * scale + shift).astype(BF16)


def call(kernel, out_shape, in_specs, scratch=(), megabytes=4, flops=0, moved=0):
    return pl.pallas_call(
        kernel,
        out_shape=out_shape,
        in_specs=in_specs,
        out_specs=jax.tree.map(lambda _: VMEM, out_shape),
        scratch_shapes=list(scratch),
        compiler_params=pltpu.CompilerParams(vmem_limit_bytes=megabytes << 20),
        cost_estimate=pl.CostEstimate(flops=flops, bytes_accessed=moved, transcendentals=0),
    )


def passed_on(array, tm_by, band_by):
    tms, bands = lax.axis_size("tm"), lax.axis_size("band")
    pairs = [
        (i * bands + b, (i + tm_by) % tms * bands + (b + band_by) % bands)
        for i in range(tms)
        for b in range(bands)
    ]
    return lax.ppermute(array, ("tm", "band"), pairs)


def on_device(
    frames_in, clip_id, conv_weight, conv_bias, norm_gain, norm_shift, down_weight, out_gain, out_shift
):
    frames, rows, cols, channels = frames_in.shape
    wide = down_weight.shape[-1]
    bands = lax.axis_size("band")
    devices, half, lines = lax.axis_size("tm") * bands, cols // 2, rows // 2
    shape = jax.ShapeDtypeStruct
    everyone = shape((devices, 1, 128), F32)

    def exchange(row):
        return lax.all_to_all(row, ("tm", "band"), 0, 0, tiled=True).reshape(devices, 128)

    before = passed_on(frames_in, 1, 0)
    row, top, bottom = call(
        sums_kernel,
        (
            everyone,
            shape((frames, 2, cols, channels), BF16),
            shape((frames, 1, cols, channels), BF16),
        ),
        [VMEM],
        flops=1 << 33,
        moved=1 << 20,
    )(frames_in)
    below_before, below = passed_on(top, 1, -1), passed_on(top, 0, -1)
    above_before, above = passed_on(bottom, 1, 1), passed_on(bottom, 0, 1)
    sums = exchange(row)
    down = down_weight.reshape(-1, wide)
    pair = (half, 2 * channels)
    residual, partial, info = call(
        functools.partial(conv_kernel, bands, float(bands * rows * cols * (channels // GROUPS))),
        (
            shape((frames, rows + 1, *pair), BF16),
            shape((frames, lines, half, wide), BF16),
            shape((8, 128), jnp.int32),
        ),
        [VMEM] * 13,
        scratch=[
            pltpu.VMEM((4, rows + 3, *pair), BF16),
            pltpu.VMEM((frames, rows + 1, *pair), BF16),
            pltpu.VMEM((9, 2 * channels, 4 * channels), BF16),
            pltpu.VMEM((rows + 3, cols, channels), F32),
        ],
        megabytes=28,
        flops=5 << 30,
        moved=1 << 23,
    )(
        sums, clip_id.reshape(1, -1), conv_bias.reshape(1, -1), norm_gain.reshape(1, -1),
        norm_shift.reshape(1, -1), conv_weight.reshape(9, 3, channels, channels), down,
        frames_in, before, above, above_before, below, below_before,
    )
    arrived = passed_on(partial, 1, 0)
    local = call(
        local_kernel,
        shape((frames, lines, half, wide), F32),
        [VMEM] * 3,
        megabytes=16,
        flops=1 << 31,
        moved=1 << 22,
    )(info, residual, down)
    reduced, row = call(
        join_kernel,
        (shape((frames, lines, half, wide), BF16), everyone),
        [VMEM] * 2,
        megabytes=8,
        moved=1 << 21,
    )(local, arrived)
    return call(
        functools.partial(out_kernel, bands, float(bands * lines * half * (wide // GROUPS))),
        shape((frames, lines, half, wide), BF16),
        [VMEM] * 5,
        megabytes=8,
        moved=1 << 20,
    )(exchange(row), info, out_gain.reshape(1, -1), out_shift.reshape(1, -1), reduced)


def solution(mesh):
    return jax.shard_map(
        on_device,
        mesh=mesh,
        in_specs=(P("tm", "band", None, None), P(), P(), P(), P(), P(), P(), P(), P()),
        out_specs=P("tm", "band", None, None),
        check_vma=False,
    )
```

```python
import functools
import jax
import jax.numpy as jnp
from jax import lax
from jax.experimental import pallas as pl
from jax.experimental.pallas import tpu as pltpu
from jax.sharding import PartitionSpec as P

GROUPS = 32
EPS = 1e-06
F32 = jnp.float32
BF16 = jnp.bfloat16
VMEM = pl.BlockSpec(memory_space=pltpu.VMEM)
cat = jnp.concatenate


def iota(shape, dim):
    return lax.broadcasted_iota(jnp.int32, shape, dim)


def exact_dot(rows, zero_one):
    n = rows.shape[0]
    high = rows.astype(BF16)
    rest = rows - high.astype(F32)
    middle = rest.astype(BF16)
    low = (rest - middle.astype(F32)).astype(BF16)
    parts = cat([high.astype(F32), middle.astype(F32), low.astype(F32)], axis=0)
    spare = -parts.shape[0] % 16
    if spare:
        parts = cat([parts, jnp.zeros((spare, parts.shape[1]), F32)], axis=0)
    found = jnp.dot(parts.astype(BF16), zero_one.astype(BF16), preferred_element_type=F32)
    return found[:n] + found[n : 2 * n] + found[2 * n : 3 * n]


def pack_row(sums):
    channels = sums[0].shape[1]
    size = channels // GROUPS
    gather = iota((channels, 128), 0) // size == iota((channels, 128), 1) % GROUPS
    grouped = exact_dot(cat(sums, axis=0), gather.astype(F32))
    place = iota((4, 128), 1) // GROUPS == iota((4, 128), 0)
    return jnp.sum(jnp.where(place, grouped, 0.0), axis=0, keepdims=True)


def frame_sums(lines):
    deep = 64
    channels = lines[0].shape[1]
    one, two = jnp.zeros((deep, channels), F32), jnp.zeros((deep, channels), F32)
    for v in lines:
        for a in range(0, v.shape[0], deep):
            part = v[a : a + deep]
            one, two = one + part, two + part * part
    return [jnp.sum(one, axis=0, keepdims=True), jnp.sum(two, axis=0, keepdims=True)]


def scale_and_shift(rows, info_ref, gain, offset, cells, bands):
    channels = gain.shape[1]
    size = channels // GROUPS
    frame = 2 * (iota(rows.shape, 0) // bands) + iota(rows.shape, 1) // 64
    lane, channel = iota((128, 2 * channels), 0) % 64, iota((128, 2 * channels), 1)
    spread = lane == GROUPS * (channel // channels) + channel % channels // size
    totals = []
    for n in range(2):
        begin, end = info_ref[n : n + 1, :], info_ref[4 + n : 5 + n, :]
        inside = jnp.where((frame >= begin) & (frame < end), rows, 0.0)
        totals.append(jnp.sum(inside, axis=0, keepdims=True))
    sums = exact_dot(cat(totals, axis=0), spread.astype(F32))
    found = []
    for n in range(2):
        frames = (info_ref[4 + n : 5 + n, :] - info_ref[n : n + 1, :]).astype(F32)
        per = 1.0 / (cat([frames] * (channels // 128), axis=1) * cells)
        mean = sums[n : n + 1, :channels] * per
        inv_std = lax.rsqrt(sums[n : n + 1, channels:] * per - mean * mean + EPS)
        scale = inv_std * gain
        found.append((scale, offset - mean * scale))
    return found


def sums_kernel(x_ref, row_ref, top_ref, bottom_ref):
    frames, rows = x_ref.shape[:2]
    top_ref[...] = x_ref[:, 0:2]
    bottom_ref[...] = x_ref[:, rows - 1 : rows]
    sums = []
    for f in range(frames):
        sums += frame_sums([x_ref[f, r].astype(F32) for r in range(rows)])
    row_ref[...] = jnp.broadcast_to(pack_row(sums)[None], row_ref.shape)


def arrange(weight_ref, weights):
    channels = weight_ref.shape[2]
    zero = jnp.zeros((channels, channels), BF16)
    for tap in range(9):
        w0, w1, w2 = (weight_ref[tap, dx] for dx in range(3))
        weights[tap, 0:channels] = cat([w1, w0, zero, w2], axis=1)
        weights[tap, channels : 2 * channels] = cat([w2, w1, w0, zero], axis=1)


def clip_table(clip_ref, first):
    ids = clip_ref[...].astype(F32)
    lane = iota(ids.shape, 1)
    begins, ends = [], []
    for n in range(4):
        at = jnp.minimum(first + n, ids.shape[1] - 1)
        mine = jnp.sum(jnp.where(lane == at, ids, 0.0), axis=1, keepdims=True)
        begins.append(jnp.sum(jnp.where(ids < mine, 1.0, 0.0), axis=1, keepdims=True))
        ends.append(jnp.sum(jnp.where(ids <= mine, 1.0, 0.0), axis=1, keepdims=True))
    return cat([jnp.broadcast_to(v, (1, 128)) for v in begins + ends], axis=0).astype(jnp.int32)


def activated(value, scale, shift):
    u = value.astype(F32) * scale + shift
    return u + u * jnp.tanh(u)


def convolve(line, weights_ref, outputs):
    weights = weights_ref[...].reshape(-1, weights_ref.shape[2])
    window = cat(
        [
            cat([line(sources[k], r + dy) for sources, r in outputs], axis=0)
            for k in range(3)
            for dy in (-1, 0, 1)
        ],
        axis=1,
    )
    found = jnp.dot(window, weights, preferred_element_type=F32)
    wide = found.shape[1] // 2
    channels = wide // 2
    size = found.shape[0]
    half = size // len(outputs)
    column = iota((size, channels), 0) % half
    from_left = jnp.where(column == 0, 0.0, pltpu.roll(found[:, wide : wide + channels], 1, 0))
    from_right = jnp.where(column == half - 1, 0.0, pltpu.roll(found[:, wide + channels :], size - 1, 0))
    total = found[:, :wide] + cat([from_left, from_right], axis=1)
    return [total[n * half : (n + 1) * half] for n in range(len(outputs))]


def strided(lines, down_ref, k):
    wide = down_ref.shape[1]
    channels = down_ref.shape[0] // 27
    windows = [lines(dy) for dy in range(3)]
    half = windows[0].shape[1]
    windows = [w.reshape(-1, wide) for w in windows]
    places = [(k * 9 + dy * 3) * channels for dy in range(3)]
    both = cat([down_ref[at : at + 2 * channels] for at in places], axis=0)
    next_even = cat([down_ref[at + 2 * channels : at + 3 * channels] for at in places], axis=0)
    total = jnp.dot(cat(windows, axis=1), both, preferred_element_type=F32)
    shifted = jnp.dot(
        cat([w[:, :channels] for w in windows], axis=1), next_even, preferred_element_type=F32
    )
    size = total.shape[0]
    column = iota(shifted.shape, 0) % half
    shifted = jnp.where(column == half - 1, 0.0, pltpu.roll(shifted, size - 1, 0))
    return (total + shifted).reshape(-1, half, wide)


def hand_on(line, outputs, info_ref, first, down_ref, partial_ref):
    begins = [info_ref[2, 0], info_ref[3, 0]]
    source = (begins[0] > first).astype(jnp.int32)
    takes = [(b <= first + 1).astype(F32) for b in begins]

    def both(dy):
        return jnp.stack([line(f, 2 * i + dy) for f in (source, 1) for i in outputs])

    def second(dy):
        return jnp.stack([line(1, 2 * i + dy) for i in outputs])

    n = len(outputs)
    older = strided(both, down_ref, 0)
    newer = strided(second, down_ref, 1)
    partial_ref[0] = ((older[:n] + newer) * takes[0]).astype(BF16)
    partial_ref[1] = (older[n:] * takes[1]).astype(BF16)


def frame_sources(info_ref, first):
    return [
        [jnp.maximum(first + f - 2 + k, info_ref[f, 0]) - (first - 2) for k in range(3)] for f in range(2)
    ]


def conv_first_kernel(which, bands, cells, clip_ref, *refs):
    ins, (residual_ref, partial_ref, info_ref), scratch = refs[:12], refs[12:15], refs[15:]
    info_ref[...] = clip_table(clip_ref, lax.axis_index("tm") * 2)
    conv_kernel(which, bands, cells, info_ref, *ins, residual_ref, partial_ref, *scratch)


def conv_kernel(which, bands, cells, *refs):
    @pl.when(lax.axis_index("tm") % 2 == which)
    def _():
        convolve_frames(bands, cells, *refs)


def convolve_frames(
    bands, cells, info_ref, rows_ref, bias_ref, gain_ref, offset_ref, weight_ref, down_ref,
    x_ref, before_ref, above_ref, above_before_ref, below_ref, below_before_ref,
    residual_ref, partial_ref, hidden, own, weights, slots,
):
    rows, cols, channels = x_ref.shape[1:]
    first = lax.axis_index("tm") * 2
    band = lax.axis_index("band")
    keep_above = (band > 0).astype(F32)
    keep_below = (band < bands - 1).astype(F32)
    arrange(weight_ref, weights)
    bias = bias_ref[...]
    stats = scale_and_shift(rows_ref[...], info_ref, gain_ref[...], offset_ref[...], cells, bands)
    stats = [0.5 * v for pair in stats for v in pair]
    for frame in range(4):
        scale, shift = stats[2:] if frame == 3 else stats[:2]
        body, above, below = (
            (before_ref, above_before_ref, below_before_ref)
            if frame < 2
            else (x_ref, above_ref, below_ref)
        )
        f = frame % 2
        lines = [above.at[f, 0]] + [body.at[f, r] for r in range(rows)] + [below.at[f, r] for r in range(2)]
        for n, line in enumerate(lines):
            slot = slots.at[n]
            slot[...] = line[...].astype(F32)
            for side in range(2):
                lanes = pl.ds(side * channels, channels)
                value = slot[pl.ds(side, cols // 2, 2), :]
                if frame >= 2 and 1 <= n < rows + 2:
                    own[f, n - 1, :, lanes] = value.astype(BF16)
                value = activated(value, scale, shift)
                if n == 0:
                    value = value * keep_above
                if n > rows:
                    value = value * keep_below
                hidden[frame, n, :, lanes] = value.astype(BF16)
    sources = frame_sources(info_ref, first)
    bias = cat([bias, bias], axis=1)
    for f in range(2):
        found = convolve(
            lambda source, r: hidden[source, r + 1], weights, [(sources[f], r) for r in range(rows + 1)]
        )
        for r, total in enumerate(found):
            value = total + own[f, r].astype(F32) + bias
            if r == rows:
                value = value * keep_below
            residual_ref[f, r] = value.astype(BF16)
    hand_on(
        lambda f, r: residual_ref[f, r], range(rows // 2), info_ref, first, down_ref, partial_ref
    )


def local_kernel(info_ref, first_core_ref, second_core_ref, down_ref, out_ref):
    for which, residual_ref in enumerate((first_core_ref, second_core_ref)):

        @pl.when(lax.axis_index("tm") % 2 == which)
        def _(residual_ref=residual_ref):
            local_part(info_ref, residual_ref, down_ref, out_ref)


def local_part(info_ref, residual_ref, down_ref, out_ref):
    first = lax.axis_index("tm") * 2
    begins = [info_ref[0, 0], info_ref[1, 0]]
    count = out_ref.shape[1]

    def lines(*picked):
        return lambda dy: jnp.stack([residual_ref[f, 2 * i + dy] for f in picked for i in range(count)])

    base = strided(lines(0, 1), down_ref, 2)
    out_ref[0] = base[:count]
    out_ref[1] = base[count:] + strided(lines((begins[1] > first).astype(jnp.int32)), down_ref, 1)

    @pl.when(begins[0] == first)
    def _():
        out_ref[0] += strided(lines(0), down_ref, 0) + strided(lines(0), down_ref, 1)

    @pl.when(begins[1] >= first)
    def _():
        out_ref[1] += strided(lines(begins[1] - first), down_ref, 0)


def join_kernel(local_ref, between_ref, within_ref, reduced_ref, row_ref):
    frames, lines, half, channels = local_ref.shape
    sums = []
    for f in range(frames):
        values = []
        for i in range(lines):
            sent = between_ref[f, i].astype(F32) + within_ref[f, i].astype(F32)
            v = (local_ref[f, i] + sent).astype(BF16)
            reduced_ref[f, i] = v
            values.append(v.astype(F32))
        sums += frame_sums(values)
    row_ref[...] = jnp.broadcast_to(pack_row(sums)[None], row_ref.shape)


def out_kernel(bands, cells, rows_ref, info_ref, gain_ref, offset_ref, reduced_ref, out_ref):
    frames, lines = reduced_ref.shape[:2]
    stats = scale_and_shift(rows_ref[...], info_ref, gain_ref[...], offset_ref[...], cells, bands)
    for f in range(frames):
        scale, shift = stats[f]
        for i in range(lines):
            out_ref[f, i] = (reduced_ref[f, i].astype(F32) * scale + shift).astype(BF16)


def call(kernel, out_shape, in_specs, scratch=(), megabytes=4, flops=0, moved=0):
    return pl.pallas_call(
        kernel,
        out_shape=out_shape,
        in_specs=in_specs,
        out_specs=jax.tree.map(lambda _: VMEM, out_shape),
        scratch_shapes=list(scratch),
        compiler_params=pltpu.CompilerParams(vmem_limit_bytes=megabytes << 20),
        cost_estimate=pl.CostEstimate(flops=flops, bytes_accessed=moved, transcendentals=0),
    )


def passed_on(array, tm_by, band_by):
    tms, bands = lax.axis_size("tm"), lax.axis_size("band")
    pairs = [
        (i * bands + b, (i + tm_by) % tms * bands + (b + band_by) % bands)
        for i in range(tms)
        for b in range(bands)
    ]
    return lax.ppermute(array, ("tm", "band"), pairs)


def between_chips(array):
    return lax.ppermute(array, "tm", [(i, i + 1) for i in range(1, lax.axis_size("tm") - 1, 2)])


def within_chips(array):
    return lax.ppermute(array, "tm", [(i, i + 1) for i in range(0, lax.axis_size("tm"), 2)])


def on_device(
    frames_in, clip_id, conv_weight, conv_bias, norm_gain, norm_shift, down_weight, out_gain, out_shift
):
    frames, rows, cols, channels = frames_in.shape
    wide = down_weight.shape[-1]
    bands = lax.axis_size("band")
    devices, half, lines = lax.axis_size("tm") * bands, cols // 2, rows // 2
    shape = jax.ShapeDtypeStruct
    everyone = shape((devices, 1, 128), F32)

    def exchange(row):
        return lax.all_to_all(row, ("tm", "band"), 0, 0, tiled=True).reshape(devices, 128)

    before = passed_on(frames_in, 1, 0)
    row, top, bottom = call(
        sums_kernel,
        (
            everyone,
            shape((frames, 2, cols, channels), BF16),
            shape((frames, 1, cols, channels), BF16),
        ),
        [VMEM],
        flops=1 << 33,
        moved=1 << 20,
    )(frames_in)
    below_before, below = passed_on(top, 1, -1), passed_on(top, 0, -1)
    above_before, above = passed_on(bottom, 1, 1), passed_on(bottom, 0, 1)
    sums = exchange(row)
    down = down_weight.reshape(-1, wide)
    pair = (half, 2 * channels)
    def conv(kernel, which, info, *more):
        cells = float(bands * rows * cols * (channels // GROUPS))
        return call(
            functools.partial(kernel, which, bands, cells),
            (shape((frames, rows + 1, *pair), BF16), shape((frames, lines, half, wide), BF16), *more),
            [VMEM] * 13,
            scratch=[
                pltpu.VMEM((4, rows + 3, *pair), BF16),
                pltpu.VMEM((frames, rows + 1, *pair), BF16),
                pltpu.VMEM((9, 2 * channels, 4 * channels), BF16),
                pltpu.VMEM((rows + 3, cols, channels), F32),
            ],
            megabytes=24,
            flops=5 << 30,
            moved=1 << 23,
        )(
            info, sums, conv_bias.reshape(1, -1), norm_gain.reshape(1, -1),
            norm_shift.reshape(1, -1), conv_weight.reshape(9, 3, channels, channels), down,
            frames_in, before, above, above_before, below, below_before,
        )

    second_core, partial, info = conv(
        conv_first_kernel, 1, clip_id.reshape(1, -1), shape((8, 128), jnp.int32)
    )
    between = between_chips(partial)
    first_core, partial = conv(conv_kernel, 0, info)
    within = within_chips(partial)
    local = call(
        local_kernel,
        shape((frames, lines, half, wide), F32),
        [VMEM] * 4,
        megabytes=12,
        flops=1 << 31,
        moved=1 << 22,
    )(info, first_core, second_core, down)
    reduced, row = call(
        join_kernel,
        (shape((frames, lines, half, wide), BF16), everyone),
        [VMEM] * 3,
        megabytes=8,
        moved=1 << 21,
    )(local, between, within)
    return call(
        functools.partial(out_kernel, bands, float(bands * lines * half * (wide // GROUPS))),
        shape((frames, lines, half, wide), BF16),
        [VMEM] * 5,
        megabytes=8,
        moved=1 << 20,
    )(exchange(row), info, out_gain.reshape(1, -1), out_shift.reshape(1, -1), reduced)


def solution(mesh):
    return jax.shard_map(
        on_device,
        mesh=mesh,
        in_specs=(P("tm", "band", None, None), P(), P(), P(), P(), P(), P(), P(), P()),
        out_specs=P("tm", "band", None, None),
        check_vma=False,
    )
```

```python
import functools
import jax
import jax.numpy as jnp
from jax import lax
from jax.experimental import pallas as pl
from jax.experimental.pallas import tpu as pltpu
from jax.sharding import PartitionSpec as P

GROUPS = 32
EPS = 1e-06
F32 = jnp.float32
BF16 = jnp.bfloat16
VMEM = pl.BlockSpec(memory_space=pltpu.VMEM)
cat = jnp.concatenate


def iota(shape, dim):
    return lax.broadcasted_iota(jnp.int32, shape, dim)


def exact_dot(rows, zero_one):
    n = rows.shape[0]
    high = rows.astype(BF16)
    rest = rows - high.astype(F32)
    middle = rest.astype(BF16)
    low = (rest - middle.astype(F32)).astype(BF16)
    parts = cat([high.astype(F32), middle.astype(F32), low.astype(F32)], axis=0)
    spare = -parts.shape[0] % 16
    if spare:
        parts = cat([parts, jnp.zeros((spare, parts.shape[1]), F32)], axis=0)
    found = jnp.dot(parts.astype(BF16), zero_one.astype(BF16), preferred_element_type=F32)
    return found[:n] + found[n : 2 * n] + found[2 * n : 3 * n]


def pack_row(sums):
    channels = sums[0].shape[1]
    size = channels // GROUPS
    gather = iota((channels, 128), 0) // size == iota((channels, 128), 1) % GROUPS
    grouped = exact_dot(cat(sums, axis=0), gather.astype(F32))
    place = iota((4, 128), 1) // GROUPS == iota((4, 128), 0)
    return jnp.sum(jnp.where(place, grouped, 0.0), axis=0, keepdims=True)


def frame_sums(lines):
    deep = 64
    channels = lines[0].shape[1]
    one, two = jnp.zeros((deep, channels), F32), jnp.zeros((deep, channels), F32)
    for v in lines:
        for a in range(0, v.shape[0], deep):
            part = v[a : a + deep]
            one, two = one + part, two + part * part
    return [jnp.sum(one, axis=0, keepdims=True), jnp.sum(two, axis=0, keepdims=True)]


def scale_and_shift(rows, info_ref, gain, offset, cells, bands):
    channels = gain.shape[1]
    size = channels // GROUPS
    frame = 2 * (iota(rows.shape, 0) // bands) + iota(rows.shape, 1) // 64
    lane, channel = iota((128, 2 * channels), 0) % 64, iota((128, 2 * channels), 1)
    spread = lane == GROUPS * (channel // channels) + channel % channels // size
    totals = []
    for n in range(2):
        begin, end = info_ref[n : n + 1, :], info_ref[4 + n : 5 + n, :]
        inside = jnp.where((frame >= begin) & (frame < end), rows, 0.0)
        totals.append(jnp.sum(inside, axis=0, keepdims=True))
    sums = exact_dot(cat(totals, axis=0), spread.astype(F32))
    found = []
    for n in range(2):
        frames = (info_ref[4 + n : 5 + n, :] - info_ref[n : n + 1, :]).astype(F32)
        per = 1.0 / (cat([frames] * (channels // 128), axis=1) * cells)
        mean = sums[n : n + 1, :channels] * per
        inv_std = lax.rsqrt(sums[n : n + 1, channels:] * per - mean * mean + EPS)
        scale = inv_std * gain
        found.append((scale, offset - mean * scale))
    return found


def sums_kernel(x_ref, row_ref, top_ref):
    frames, rows = x_ref.shape[:2]
    top_ref[...] = x_ref[:, 0:2]
    sums = []
    for f in range(frames):
        sums += frame_sums([x_ref[f, r].astype(F32) for r in range(rows)])
    row_ref[...] = jnp.broadcast_to(pack_row(sums)[None], row_ref.shape)


def arrange(weight_ref, weights):
    channels = weight_ref.shape[2]
    zero = jnp.zeros((channels, channels), BF16)
    for tap in range(9):
        w0, w1, w2 = (weight_ref[tap, dx] for dx in range(3))
        weights[tap, 0:channels] = cat([w1, w0, zero, w2], axis=1)
        weights[tap, channels : 2 * channels] = cat([w2, w1, w0, zero], axis=1)


def clip_table(clip_ref, first):
    ids = clip_ref[...].astype(F32)
    lane = iota(ids.shape, 1)
    begins, ends = [], []
    for n in range(4):
        at = jnp.minimum(first + n, ids.shape[1] - 1)
        mine = jnp.sum(jnp.where(lane == at, ids, 0.0), axis=1, keepdims=True)
        begins.append(jnp.sum(jnp.where(ids < mine, 1.0, 0.0), axis=1, keepdims=True))
        ends.append(jnp.sum(jnp.where(ids <= mine, 1.0, 0.0), axis=1, keepdims=True))
    return cat([jnp.broadcast_to(v, (1, 128)) for v in begins + ends], axis=0).astype(jnp.int32)


def activated(value, scale, shift):
    u = value.astype(F32) * scale + shift
    return u + u * jnp.tanh(u)


def convolve(line, weights_ref, outputs):
    weights = weights_ref[...].reshape(-1, weights_ref.shape[2])
    window = cat(
        [
            cat([line(sources[k], r, dy) for sources, r in outputs], axis=0)
            for k in range(3)
            for dy in (-1, 0, 1)
        ],
        axis=1,
    )
    found = jnp.dot(window, weights, preferred_element_type=F32)
    wide = found.shape[1] // 2
    channels = wide // 2
    size = found.shape[0]
    half = size // len(outputs)
    column = iota((size, channels), 0) % half
    from_left = jnp.where(column == 0, 0.0, pltpu.roll(found[:, wide : wide + channels], 1, 0))
    from_right = jnp.where(column == half - 1, 0.0, pltpu.roll(found[:, wide + channels :], size - 1, 0))
    total = found[:, :wide] + cat([from_left, from_right], axis=1)
    return [total[n * half : (n + 1) * half] for n in range(len(outputs))]


def from_right(value, half):
    column = iota(value.shape, 0) % half
    return jnp.where(column == half - 1, 0.0, pltpu.roll(value, value.shape[0] - 1, 0))


def tap_weights(down_ref, k, dy):
    channels = down_ref.shape[0] // 27
    at = (k * 9 + dy * 3) * channels
    return down_ref[at : at + 2 * channels], down_ref[at + 2 * channels : at + 3 * channels]


def strided(residual_ref, frames, down_ref, k):
    rows, half, wide = residual_ref.shape[1] - 1, *residual_ref.shape[2:]
    channels = wide // 2

    def lines(picked):
        return cat([residual_ref[f, r - 1] for f in frames for r in picked], axis=0)

    zero, one = lines(range(2, rows, 2)), lines(range(1, rows, 2))
    two = lines([*range(2, rows, 2), rows + 1])
    (both_0, next_0), (both_1, next_1), (both_2, next_2) = (tap_weights(down_ref, k, dy) for dy in range(3))
    dot = functools.partial(jnp.dot, preferred_element_type=F32)
    total = dot(cat([one, two], axis=1), cat([both_1, both_2], axis=0))
    evens = cat([one[:, :channels], two[:, :channels]], axis=1)
    total = total + from_right(dot(evens, cat([next_1, next_2], axis=0)), half)
    upper = dot(zero, both_0) + from_right(dot(zero[:, :channels], next_0), half)
    total = total.reshape(len(frames), rows // 2, half, -1)
    upper = upper.reshape(len(frames), rows // 2 - 1, half, -1)
    return cat([total[:, :1], total[:, 1:] + upper], axis=1)


def hand_on(residual_ref, info_ref, first, down_ref, partial_ref):
    begins = [info_ref[2, 0], info_ref[3, 0]]
    source = (begins[0] > first).astype(jnp.int32)
    takes = [(b <= first + 1).astype(F32) for b in begins]
    older = strided(residual_ref, (source, 1), down_ref, 0)
    newer = strided(residual_ref, (1,), down_ref, 1)
    partial_ref[0] = ((older[0] + newer[0]) * takes[0]).astype(BF16)
    partial_ref[1] = (older[1] * takes[1]).astype(BF16)


def frame_sources(info_ref, first):
    return [
        [jnp.maximum(first + f - 2 + k, info_ref[f, 0]) - (first - 2) for k in range(3)] for f in range(2)
    ]


def on_core(which):
    return pl.when(lax.axis_index("tm") % 2 == which)


def second_core_kernel(bands, cells, down_ref, clip_ref, *refs):
    ins, (residual_ref, edge_ref, partial_ref, info_ref), scratch = refs[:9], refs[9:13], refs[13:]
    first = lax.axis_index("tm") * 2
    info_ref[...] = clip_table(clip_ref, first)

    @on_core(1)
    def _():
        convolve_frames(bands, cells, info_ref, *ins, residual_ref, edge_ref, *scratch)
        hand_on(residual_ref, info_ref, first, down_ref, partial_ref)


def first_core_kernel(bands, cells, other_edge_ref, info_ref, *refs):
    ins, (residual_ref, edge_ref), scratch = refs[:9], refs[9:11], refs[11:]

    @on_core(0)
    def _():
        convolve_frames(bands, cells, info_ref, *ins, residual_ref, edge_ref, *scratch)

    @on_core(1)
    def _():
        edge_ref[...] = other_edge_ref[...]


def convolve_frames(
    bands, cells, info_ref, rows_ref, bias_ref, gain_ref, offset_ref, weight_ref,
    x_ref, before_ref, below_ref, below_before_ref,
    residual_ref, edge_ref, hidden, own, weights, slots,
):
    rows, cols, channels = x_ref.shape[1:]
    first = lax.axis_index("tm") * 2
    keep = (lax.axis_index("band") < bands - 1).astype(F32)
    arrange(weight_ref, weights)
    bias = bias_ref[...]
    stats = scale_and_shift(rows_ref[...], info_ref, gain_ref[...], offset_ref[...], cells, bands)
    stats = [0.5 * v for pair in stats for v in pair]
    for frame in range(4):
        scale, shift = stats[2:] if frame == 3 else stats[:2]
        body, below = (before_ref, below_before_ref) if frame < 2 else (x_ref, below_ref)
        f = frame % 2
        lines = [body.at[f, r] for r in range(rows)] + [below.at[f, r] for r in range(2)]
        for n, line in enumerate(lines):
            slot = slots.at[n]
            slot[...] = line[...].astype(F32)
            for side in range(2):
                lanes = pl.ds(side * channels, channels)
                value = slot[pl.ds(side, cols // 2, 2), :]
                if frame >= 2 and 1 <= n <= rows:
                    own[f, n - 1, :, lanes] = value.astype(BF16)
                value = activated(value, scale, shift)
                hidden[frame, n, :, lanes] = value.astype(BF16)
                if n in (rows - 1, rows):
                    hidden[frame, n + 3, :, lanes] = (value * keep).astype(BF16)

    def line(source, r, dy):
        across = (r, dy) in ((rows - 1, 1), (rows, -1))
        return hidden[source, r + dy + (3 if across else 0)]

    sources = frame_sources(info_ref, first)
    bias = cat([bias, bias], axis=1)
    for f in range(2):
        found = convolve(line, weights, [(sources[f], r) for r in range(1, rows + 1)])
        for n, total in enumerate(found):
            value = total + own[f, n].astype(F32) + bias
            residual_ref[f, n] = value.astype(BF16)
            if n == rows - 1:
                residual_ref[f, rows] = (value * keep).astype(BF16)
                edge_ref[f] = value.astype(BF16)


def hand_on_kernel(info_ref, residual_ref, down_ref, partial_ref):
    @on_core(0)
    def _():
        hand_on(residual_ref, info_ref, lax.axis_index("tm") * 2, down_ref, partial_ref)


def local_kernel(info_ref, first_core_ref, second_core_ref, down_ref, out_ref):
    for which, residual_ref in enumerate((first_core_ref, second_core_ref)):

        @on_core(which)
        def _(residual_ref=residual_ref):
            local_part(info_ref, residual_ref, down_ref, out_ref)


def local_part(info_ref, residual_ref, down_ref, out_ref):
    first = lax.axis_index("tm") * 2
    begins = [info_ref[0, 0], info_ref[1, 0]]
    base = strided(residual_ref, (0, 1), down_ref, 2)
    out_ref[0] = base[0]
    out_ref[1] = base[1] + strided(residual_ref, ((begins[1] > first).astype(jnp.int32),), down_ref, 1)[0]

    @pl.when(begins[0] == first)
    def _():
        out_ref[0] += strided(residual_ref, (0,), down_ref, 0)[0] + strided(residual_ref, (0,), down_ref, 1)[0]

    @pl.when(begins[1] >= first)
    def _():
        out_ref[1] += strided(residual_ref, (begins[1] - first,), down_ref, 0)[0]


def row_zero_kernel(info_ref, edge_before_ref, edge_ref, down_ref, out_ref, four):
    half, wide = edge_ref.shape[1:]
    four[0:2] = edge_before_ref[...]
    four[2:4] = edge_ref[...]
    sources = frame_sources(info_ref, lax.axis_index("tm") * 2)
    weights = [tap_weights(down_ref, k, 0) for k in range(3)]
    lines = cat([cat([four[s] for s in sources[f]], axis=1) for f in range(2)], axis=0)
    evens = cat([lines[:, k * wide : k * wide + wide // 2] for k in range(3)], axis=1)
    total = jnp.dot(lines, cat([w[0] for w in weights], axis=0), preferred_element_type=F32)
    shifted = jnp.dot(evens, cat([w[1] for w in weights], axis=0), preferred_element_type=F32)
    out_ref[...] = (total + from_right(shifted, half)).reshape(out_ref.shape)


def first_line_kernel(upper_ref, local_ref, between_ref, out_ref):
    out_ref[...] = upper_ref[...] + local_ref[:, 0] + between_ref[:, 0].astype(F32)


def join_kernel(first_line_ref, local_ref, between_ref, within_ref, reduced_ref, row_ref):
    frames, lines = local_ref.shape[:2]
    sums = []
    for f in range(frames):
        values = []
        for i in range(lines):
            v = first_line_ref[f] if i == 0 else local_ref[f, i] + between_ref[f, i].astype(F32)
            v = (v + within_ref[f, i].astype(F32)).astype(BF16)
            reduced_ref[f, i] = v
            values.append(v.astype(F32))
        sums += frame_sums(values)
    row_ref[...] = jnp.broadcast_to(pack_row(sums)[None], row_ref.shape)


def out_kernel(bands, cells, rows_ref, info_ref, gain_ref, offset_ref, reduced_ref, out_ref):
    frames, lines = reduced_ref.shape[:2]
    stats = scale_and_shift(rows_ref[...], info_ref, gain_ref[...], offset_ref[...], cells, bands)
    for f in range(frames):
        scale, shift = stats[f]
        for i in range(lines):
            out_ref[f, i] = (reduced_ref[f, i].astype(F32) * scale + shift).astype(BF16)


def call(kernel, out_shape, in_specs, scratch=(), megabytes=4, flops=0, moved=0):
    return pl.pallas_call(
        kernel,
        out_shape=out_shape,
        in_specs=in_specs,
        out_specs=jax.tree.map(lambda _: VMEM, out_shape),
        scratch_shapes=list(scratch),
        compiler_params=pltpu.CompilerParams(vmem_limit_bytes=megabytes << 20),
        cost_estimate=pl.CostEstimate(flops=flops, bytes_accessed=moved, transcendentals=0),
    )


def passed_on(array, tm_by, band_by):
    tms, bands = lax.axis_size("tm"), lax.axis_size("band")
    pairs = [
        (i * bands + b, (i + tm_by) % tms * bands + (b + band_by) % bands)
        for i in range(tms)
        for b in range(bands)
    ]
    return lax.ppermute(array, ("tm", "band"), pairs)


def between_chips(array):
    return lax.ppermute(array, "tm", [(i, i + 1) for i in range(1, lax.axis_size("tm") - 1, 2)])


def within_chips(array):
    return lax.ppermute(array, "tm", [(i, i + 1) for i in range(0, lax.axis_size("tm"), 2)])


def on_device(
    frames_in, clip_id, conv_weight, conv_bias, norm_gain, norm_shift, down_weight, out_gain, out_shift
):
    frames, rows, cols, channels = frames_in.shape
    wide = down_weight.shape[-1]
    bands = lax.axis_size("band")
    devices, half, lines = lax.axis_size("tm") * bands, cols // 2, rows // 2
    shape = jax.ShapeDtypeStruct
    everyone = shape((devices, 1, 128), F32)

    def exchange(row):
        return lax.all_to_all(row, ("tm", "band"), 0, 0, tiled=True).reshape(devices, 128)

    before = passed_on(frames_in, 1, 0)
    row, top = call(
        sums_kernel,
        (everyone, shape((frames, 2, cols, channels), BF16)),
        [VMEM],
        flops=1 << 33,
        moved=1 << 20,
    )(frames_in)
    below_before, below = passed_on(top, 1, -1), passed_on(top, 0, -1)
    sums = exchange(row)
    down = down_weight.reshape(-1, wide)
    pair = (half, 2 * channels)
    def conv(kernel, given, ranges, *made):
        cells = float(bands * rows * cols * (channels // GROUPS))
        return call(
            functools.partial(kernel, bands, cells),
            (shape((frames, rows + 1, *pair), BF16), shape((frames, *pair), BF16), *made),
            [VMEM] * 11,
            scratch=[
                pltpu.VMEM((4, rows + 4, *pair), BF16),
                pltpu.VMEM((frames, rows, *pair), BF16),
                pltpu.VMEM((9, 2 * channels, 4 * channels), BF16),
                pltpu.VMEM((rows + 2, cols, channels), F32),
            ],
            megabytes=24,
            flops=5 << 30,
            moved=1 << 23,
        )(
            given, ranges, sums, conv_bias.reshape(1, -1), norm_gain.reshape(1, -1), norm_shift.reshape(1, -1),
            conv_weight.reshape(9, 3, channels, channels), frames_in, before, below, below_before,
        )

    sent = shape((frames, lines, half, wide), BF16)
    second_core, edge, partial, info = conv(
        second_core_kernel, down, clip_id.reshape(1, -1), sent, shape((8, 128), jnp.int32)
    )
    between = between_chips(partial)
    first_core, edge = conv(first_core_kernel, edge, info)
    edge, edge_before = passed_on(edge, 0, 1), passed_on(edge, 1, 1)
    partial = call(hand_on_kernel, sent, [VMEM] * 3, megabytes=12, flops=1 << 30, moved=1 << 22)(
        info, first_core, down
    )
    within = within_chips(partial)
    local = call(
        local_kernel,
        shape((frames, lines, half, wide), F32),
        [VMEM] * 4,
        megabytes=12,
        flops=1 << 31,
        moved=1 << 22,
    )(info, first_core, second_core, down)
    line = shape((frames, half, wide), F32)
    upper = call(
        row_zero_kernel, line, [VMEM] * 4, scratch=[pltpu.VMEM((4, *pair), BF16)], megabytes=6
    )(info, edge_before, edge, down)
    first_line = call(first_line_kernel, line, [VMEM] * 3, flops=1 << 32)(upper, local, between)
    reduced, row = call(
        join_kernel,
        (shape((frames, lines, half, wide), BF16), everyone),
        [VMEM] * 4,
        megabytes=8,
        moved=1 << 21,
    )(first_line, local, between, within)
    return call(
        functools.partial(out_kernel, bands, float(bands * lines * half * (wide // GROUPS))),
        shape((frames, lines, half, wide), BF16),
        [VMEM] * 5,
        megabytes=8,
        moved=1 << 20,
    )(exchange(row), info, out_gain.reshape(1, -1), out_shift.reshape(1, -1), reduced)


def solution(mesh):
    return jax.shard_map(
        on_device,
        mesh=mesh,
        in_specs=(P("tm", "band", None, None), P(), P(), P(), P(), P(), P(), P(), P()),
        out_specs=P("tm", "band", None, None),
        check_vma=False,
    )
```

```python
import functools
import jax
import jax.numpy as jnp
from jax import lax
from jax.experimental import pallas as pl
from jax.experimental.pallas import tpu as pltpu
from jax.sharding import PartitionSpec as P

GROUPS = 32
EPS = 1e-06
F32 = jnp.float32
BF16 = jnp.bfloat16
VMEM = pl.BlockSpec(memory_space=pltpu.VMEM)
cat = jnp.concatenate


def iota(shape, dim):
    return lax.broadcasted_iota(jnp.int32, shape, dim)


def exact_dot(rows, zero_one):
    n = rows.shape[0]
    high = rows.astype(BF16)
    rest = rows - high.astype(F32)
    middle = rest.astype(BF16)
    low = (rest - middle.astype(F32)).astype(BF16)
    parts = cat([high.astype(F32), middle.astype(F32), low.astype(F32)], axis=0)
    spare = -parts.shape[0] % 16
    if spare:
        parts = cat([parts, jnp.zeros((spare, parts.shape[1]), F32)], axis=0)
    found = jnp.dot(parts.astype(BF16), zero_one.astype(BF16), preferred_element_type=F32)
    return found[:n] + found[n : 2 * n] + found[2 * n : 3 * n]


def group_matrix(channels):
    size = channels // GROUPS
    return (iota((channels, 128), 0) // size == iota((channels, 128), 1) % GROUPS).astype(F32)


def matrix_kernel(out_ref):
    out_ref[...] = group_matrix(out_ref.shape[0])


def pack_row(sums, gather=None):
    channels = sums[0].shape[1]
    if gather is None:
        gather = group_matrix(channels)
    grouped = exact_dot(cat(sums, axis=0), gather)
    place = iota((4, 128), 1) // GROUPS == iota((4, 128), 0)
    return jnp.sum(jnp.where(place, grouped, 0.0), axis=0, keepdims=True)


def frame_sums(lines):
    deep = 64
    channels = lines[0].shape[1]
    one, two = jnp.zeros((deep, channels), F32), jnp.zeros((deep, channels), F32)
    for v in lines:
        for a in range(0, v.shape[0], deep):
            part = v[a : a + deep]
            one, two = one + part, two + part * part
    return [jnp.sum(one, axis=0, keepdims=True), jnp.sum(two, axis=0, keepdims=True)]


def scale_and_shift(rows, info_ref, gain, offset, cells, bands):
    channels = gain.shape[1]
    size = channels // GROUPS
    frame = 2 * (iota(rows.shape, 0) // bands) + iota(rows.shape, 1) // 64
    lane, channel = iota((128, 2 * channels), 0) % 64, iota((128, 2 * channels), 1)
    spread = lane == GROUPS * (channel // channels) + channel % channels // size
    totals = []
    for n in range(2):
        begin, end = info_ref[n : n + 1, :], info_ref[4 + n : 5 + n, :]
        inside = jnp.where((frame >= begin) & (frame < end), rows, 0.0)
        totals.append(jnp.sum(inside, axis=0, keepdims=True))
    sums = exact_dot(cat(totals, axis=0), spread.astype(F32))
    found = []
    for n in range(2):
        frames = (info_ref[4 + n : 5 + n, :] - info_ref[n : n + 1, :]).astype(F32)
        per = 1.0 / (cat([frames] * (channels // 128), axis=1) * cells)
        mean = sums[n : n + 1, :channels] * per
        inv_std = lax.rsqrt(sums[n : n + 1, channels:] * per - mean * mean + EPS)
        scale = inv_std * gain
        found.append((scale, offset - mean * scale))
    return found


def sums_kernel(x_ref, gather_ref, row_ref, top_ref):
    frames, rows = x_ref.shape[:2]
    top_ref[...] = x_ref[:, 0:2]
    sums = []
    for f in range(frames):
        sums += frame_sums([x_ref[f, r].astype(F32) for r in range(rows)])
    row_ref[...] = jnp.broadcast_to(pack_row(sums, gather_ref[...])[None], row_ref.shape)


def arrange(weight_ref, weights):
    channels = weight_ref.shape[2]
    zero = jnp.zeros((channels, channels), BF16)
    for tap in range(9):
        w0, w1, w2 = (weight_ref[tap, dx] for dx in range(3))
        weights[tap, 0:channels] = cat([w1, w0, zero, w2], axis=1)
        weights[tap, channels : 2 * channels] = cat([w2, w1, w0, zero], axis=1)


def clip_table(clip_ref, first):
    ids = clip_ref[...].astype(F32)
    lane = iota(ids.shape, 1)
    begins, ends = [], []
    for n in range(4):
        at = jnp.minimum(first + n, ids.shape[1] - 1)
        mine = jnp.sum(jnp.where(lane == at, ids, 0.0), axis=1, keepdims=True)
        begins.append(jnp.sum(jnp.where(ids < mine, 1.0, 0.0), axis=1, keepdims=True))
        ends.append(jnp.sum(jnp.where(ids <= mine, 1.0, 0.0), axis=1, keepdims=True))
    return cat([jnp.broadcast_to(v, (1, 128)) for v in begins + ends], axis=0).astype(jnp.int32)


def activated(value, scale, shift):
    u = value.astype(F32) * scale + shift
    return u + u * jnp.tanh(u)


def convolve(line, weights_ref, outputs):
    weights = weights_ref[...].reshape(-1, weights_ref.shape[2])
    window = cat(
        [
            cat([line(sources[k], r, dy) for sources, r in outputs], axis=0)
            for k in range(3)
            for dy in (-1, 0, 1)
        ],
        axis=1,
    )
    found = jnp.dot(window, weights, preferred_element_type=F32)
    wide = found.shape[1] // 2
    channels = wide // 2
    size = found.shape[0]
    half = size // len(outputs)
    column = iota((size, channels), 0) % half
    from_left = jnp.where(column == 0, 0.0, pltpu.roll(found[:, wide : wide + channels], 1, 0))
    from_right = jnp.where(column == half - 1, 0.0, pltpu.roll(found[:, wide + channels :], size - 1, 0))
    total = found[:, :wide] + cat([from_left, from_right], axis=1)
    return [total[n * half : (n + 1) * half] for n in range(len(outputs))]


def from_right(value, half):
    column = iota(value.shape, 0) % half
    return jnp.where(column == half - 1, 0.0, pltpu.roll(value, value.shape[0] - 1, 0))


def tap_weights(down_ref, k, dy):
    channels = down_ref.shape[0] // 27
    at = (k * 9 + dy * 3) * channels
    return down_ref[at : at + 2 * channels], down_ref[at + 2 * channels : at + 3 * channels]


def strided(residual_ref, frames, down_ref, k):
    rows, half, wide = residual_ref.shape[1] - 1, *residual_ref.shape[2:]
    channels = wide // 2

    def lines(picked):
        return cat([residual_ref[f, r - 1] for f in frames for r in picked], axis=0)

    zero, one = lines(range(2, rows, 2)), lines(range(1, rows, 2))
    two = lines([*range(2, rows, 2), rows + 1])
    (both_0, next_0), (both_1, next_1), (both_2, next_2) = (tap_weights(down_ref, k, dy) for dy in range(3))
    dot = functools.partial(jnp.dot, preferred_element_type=F32)
    total = dot(cat([one, two], axis=1), cat([both_1, both_2], axis=0))
    evens = cat([one[:, :channels], two[:, :channels]], axis=1)
    total = total + from_right(dot(evens, cat([next_1, next_2], axis=0)), half)
    upper = dot(zero, both_0) + from_right(dot(zero[:, :channels], next_0), half)
    total = total.reshape(len(frames), rows // 2, half, -1)
    upper = upper.reshape(len(frames), rows // 2 - 1, half, -1)
    return cat([total[:, :1], total[:, 1:] + upper], axis=1)


def hand_on(residual_ref, info_ref, first, down_ref, partial_ref):
    begins = [info_ref[2, 0], info_ref[3, 0]]
    source = (begins[0] > first).astype(jnp.int32)
    takes = [(b <= first + 1).astype(F32) for b in begins]
    older = strided(residual_ref, (source, 1), down_ref, 0)
    newer = strided(residual_ref, (1,), down_ref, 1)
    partial_ref[0] = ((older[0] + newer[0]) * takes[0]).astype(BF16)
    partial_ref[1] = (older[1] * takes[1]).astype(BF16)


def frame_sources(info_ref, first):
    return [
        [jnp.maximum(first + f - 2 + k, info_ref[f, 0]) - (first - 2) for k in range(3)] for f in range(2)
    ]


def on_core(which):
    return pl.when(lax.axis_index("tm") % 2 == which)


def second_core_kernel(bands, cells, down_ref, clip_ref, *refs):
    ins, (residual_ref, edge_ref, partial_ref, info_ref), scratch = refs[:9], refs[9:13], refs[13:]
    first = lax.axis_index("tm") * 2
    info_ref[...] = clip_table(clip_ref, first)

    @on_core(1)
    def _():
        convolve_frames(bands, cells, info_ref, *ins, residual_ref, edge_ref, *scratch)
        hand_on(residual_ref, info_ref, first, down_ref, partial_ref)


def first_core_kernel(bands, cells, other_edge_ref, info_ref, *refs):
    ins, (residual_ref, edge_ref), scratch = refs[:9], refs[9:11], refs[11:]

    @on_core(0)
    def _():
        convolve_frames(bands, cells, info_ref, *ins, residual_ref, edge_ref, *scratch)

    @on_core(1)
    def _():
        edge_ref[...] = other_edge_ref[...]


def convolve_frames(
    bands, cells, info_ref, rows_ref, bias_ref, gain_ref, offset_ref, weight_ref,
    x_ref, before_ref, below_ref, below_before_ref,
    residual_ref, edge_ref, hidden, own, weights, slots,
):
    rows, cols, channels = x_ref.shape[1:]
    first = lax.axis_index("tm") * 2
    keep = (lax.axis_index("band") < bands - 1).astype(F32)
    arrange(weight_ref, weights)
    bias = bias_ref[...]
    stats = scale_and_shift(rows_ref[...], info_ref, gain_ref[...], offset_ref[...], cells, bands)
    stats = [0.5 * v for pair in stats for v in pair]
    for frame in range(4):
        scale, shift = stats[2:] if frame == 3 else stats[:2]
        body, below = (before_ref, below_before_ref) if frame < 2 else (x_ref, below_ref)
        f = frame % 2
        lines = [body.at[f, r] for r in range(rows)] + [below.at[f, r] for r in range(2)]
        for n, line in enumerate(lines):
            slot = slots.at[n]
            slot[...] = line[...].astype(F32)
            for side in range(2):
                lanes = pl.ds(side * channels, channels)
                value = slot[pl.ds(side, cols // 2, 2), :]
                if frame >= 2 and 1 <= n <= rows:
                    own[f, n - 1, :, lanes] = value.astype(BF16)
                value = activated(value, scale, shift)
                hidden[frame, n, :, lanes] = value.astype(BF16)
                if n in (rows - 1, rows):
                    hidden[frame, n + 3, :, lanes] = (value * keep).astype(BF16)

    def line(source, r, dy):
        across = (r, dy) in ((rows - 1, 1), (rows, -1))
        return hidden[source, r + dy + (3 if across else 0)]

    sources = frame_sources(info_ref, first)
    bias = cat([bias, bias], axis=1)
    for f in range(2):
        found = convolve(line, weights, [(sources[f], r) for r in range(1, rows + 1)])
        for n, total in enumerate(found):
            value = total + own[f, n].astype(F32) + bias
            residual_ref[f, n] = value.astype(BF16)
            if n == rows - 1:
                residual_ref[f, rows] = (value * keep).astype(BF16)
                edge_ref[f] = value.astype(BF16)


def hand_on_kernel(info_ref, residual_ref, down_ref, partial_ref):
    @on_core(0)
    def _():
        hand_on(residual_ref, info_ref, lax.axis_index("tm") * 2, down_ref, partial_ref)


def local_kernel(info_ref, first_core_ref, second_core_ref, down_ref, out_ref):
    for which, residual_ref in enumerate((first_core_ref, second_core_ref)):

        @on_core(which)
        def _(residual_ref=residual_ref):
            local_part(info_ref, residual_ref, down_ref, out_ref)


def local_part(info_ref, residual_ref, down_ref, out_ref):
    first = lax.axis_index("tm") * 2
    begins = [info_ref[0, 0], info_ref[1, 0]]
    base = strided(residual_ref, (0, 1), down_ref, 2)
    out_ref[0] = base[0]
    out_ref[1] = base[1] + strided(residual_ref, ((begins[1] > first).astype(jnp.int32),), down_ref, 1)[0]

    @pl.when(begins[0] == first)
    def _():
        out_ref[0] += strided(residual_ref, (0,), down_ref, 0)[0] + strided(residual_ref, (0,), down_ref, 1)[0]

    @pl.when(begins[1] >= first)
    def _():
        out_ref[1] += strided(residual_ref, (begins[1] - first,), down_ref, 0)[0]


def row_zero_kernel(info_ref, edge_before_ref, edge_ref, down_ref, out_ref, four):
    half, wide = edge_ref.shape[1:]
    four[0:2] = edge_before_ref[...]
    four[2:4] = edge_ref[...]
    sources = frame_sources(info_ref, lax.axis_index("tm") * 2)
    weights = [tap_weights(down_ref, k, 0) for k in range(3)]
    lines = cat([cat([four[s] for s in sources[f]], axis=1) for f in range(2)], axis=0)
    evens = cat([lines[:, k * wide : k * wide + wide // 2] for k in range(3)], axis=1)
    total = jnp.dot(lines, cat([w[0] for w in weights], axis=0), preferred_element_type=F32)
    shifted = jnp.dot(evens, cat([w[1] for w in weights], axis=0), preferred_element_type=F32)
    out_ref[...] = (total + from_right(shifted, half)).reshape(out_ref.shape)


def first_line_kernel(upper_ref, local_ref, between_ref, out_ref):
    out_ref[...] = upper_ref[...] + local_ref[:, 0] + between_ref[:, 0].astype(F32)


def join_kernel(first_line_ref, local_ref, between_ref, within_ref, reduced_ref, row_ref):
    frames, lines = local_ref.shape[:2]
    sums = []
    for f in range(frames):
        values = []
        for i in range(lines):
            v = first_line_ref[f] if i == 0 else local_ref[f, i] + between_ref[f, i].astype(F32)
            v = (v + within_ref[f, i].astype(F32)).astype(BF16)
            reduced_ref[f, i] = v
            values.append(v.astype(F32))
        sums += frame_sums(values)
    row_ref[...] = jnp.broadcast_to(pack_row(sums)[None], row_ref.shape)


def out_kernel(bands, cells, rows_ref, info_ref, gain_ref, offset_ref, reduced_ref, out_ref):
    frames, lines = reduced_ref.shape[:2]
    stats = scale_and_shift(rows_ref[...], info_ref, gain_ref[...], offset_ref[...], cells, bands)
    for f in range(frames):
        scale, shift = stats[f]
        for i in range(lines):
            out_ref[f, i] = (reduced_ref[f, i].astype(F32) * scale + shift).astype(BF16)


def call(kernel, out_shape, in_specs, scratch=(), megabytes=4, flops=0, moved=0):
    return pl.pallas_call(
        kernel,
        out_shape=out_shape,
        in_specs=in_specs,
        out_specs=jax.tree.map(lambda _: VMEM, out_shape),
        scratch_shapes=list(scratch),
        compiler_params=pltpu.CompilerParams(vmem_limit_bytes=megabytes << 20),
        cost_estimate=pl.CostEstimate(flops=flops, bytes_accessed=moved, transcendentals=0),
    )


def passed_on(array, tm_by, band_by):
    tms, bands = lax.axis_size("tm"), lax.axis_size("band")
    pairs = [
        (i * bands + b, (i + tm_by) % tms * bands + (b + band_by) % bands)
        for i in range(tms)
        for b in range(bands)
    ]
    return lax.ppermute(array, ("tm", "band"), pairs)


def between_chips(array):
    return lax.ppermute(array, "tm", [(i, i + 1) for i in range(1, lax.axis_size("tm") - 1, 2)])


def within_chips(array):
    return lax.ppermute(array, "tm", [(i, i + 1) for i in range(0, lax.axis_size("tm"), 2)])


def on_device(
    frames_in, clip_id, conv_weight, conv_bias, norm_gain, norm_shift, down_weight, out_gain, out_shift
):
    frames, rows, cols, channels = frames_in.shape
    wide = down_weight.shape[-1]
    bands = lax.axis_size("band")
    devices, half, lines = lax.axis_size("tm") * bands, cols // 2, rows // 2
    shape = jax.ShapeDtypeStruct
    everyone = shape((devices, 1, 128), F32)

    def exchange(row):
        return lax.all_to_all(row, ("tm", "band"), 0, 0, tiled=True).reshape(devices, 128)

    before = passed_on(frames_in, 1, 0)
    gather = call(matrix_kernel, shape((channels, 128), F32), [], flops=1 << 29)()
    row, top = call(
        sums_kernel,
        (everyone, shape((frames, 2, cols, channels), BF16)),
        [VMEM] * 2,
        flops=1 << 33,
        moved=1 << 20,
    )(frames_in, gather)
    below_before, below = passed_on(top, 1, -1), passed_on(top, 0, -1)
    sums = exchange(row)
    down = down_weight.reshape(-1, wide)
    pair = (half, 2 * channels)
    def conv(kernel, given, ranges, *made):
        cells = float(bands * rows * cols * (channels // GROUPS))
        return call(
            functools.partial(kernel, bands, cells),
            (shape((frames, rows + 1, *pair), BF16), shape((frames, *pair), BF16), *made),
            [VMEM] * 11,
            scratch=[
                pltpu.VMEM((4, rows + 4, *pair), BF16),
                pltpu.VMEM((frames, rows, *pair), BF16),
                pltpu.VMEM((9, 2 * channels, 4 * channels), BF16),
                pltpu.VMEM((rows + 2, cols, channels), F32),
            ],
            megabytes=24,
            flops=5 << 30,
            moved=1 << 23,
        )(
            given, ranges, sums, conv_bias.reshape(1, -1), norm_gain.reshape(1, -1), norm_shift.reshape(1, -1),
            conv_weight.reshape(9, 3, channels, channels), frames_in, before, below, below_before,
        )

    sent = shape((frames, lines, half, wide), BF16)
    second_core, edge, partial, info = conv(
        second_core_kernel, down, clip_id.reshape(1, -1), sent, shape((8, 128), jnp.int32)
    )
    between = between_chips(partial)
    first_core, edge = conv(first_core_kernel, edge, info)
    edge, edge_before = passed_on(edge, 0, 1), passed_on(edge, 1, 1)
    partial = call(hand_on_kernel, sent, [VMEM] * 3, megabytes=12, flops=1 << 30, moved=1 << 22)(
        info, first_core, down
    )
    within = within_chips(partial)
    local = call(
        local_kernel,
        shape((frames, lines, half, wide), F32),
        [VMEM] * 4,
        megabytes=12,
        flops=1 << 31,
        moved=1 << 22,
    )(info, first_core, second_core, down)
    line = shape((frames, half, wide), F32)
    upper = call(
        row_zero_kernel, line, [VMEM] * 4, scratch=[pltpu.VMEM((4, *pair), BF16)], megabytes=6
    )(info, edge_before, edge, down)
    first_line = call(first_line_kernel, line, [VMEM] * 3, flops=1 << 32)(upper, local, between)
    reduced, row = call(
        join_kernel,
        (shape((frames, lines, half, wide), BF16), everyone),
        [VMEM] * 4,
        megabytes=8,
        moved=1 << 21,
    )(first_line, local, between, within)
    return call(
        functools.partial(out_kernel, bands, float(bands * lines * half * (wide // GROUPS))),
        shape((frames, lines, half, wide), BF16),
        [VMEM] * 5,
        megabytes=8,
        moved=1 << 20,
    )(exchange(row), info, out_gain.reshape(1, -1), out_shift.reshape(1, -1), reduced)


def solution(mesh):
    return jax.shard_map(
        on_device,
        mesh=mesh,
        in_specs=(P("tm", "band", None, None), P(), P(), P(), P(), P(), P(), P(), P()),
        out_specs=P("tm", "band", None, None),
        check_vma=False,
    )
```

```python
import functools
import jax
import jax.numpy as jnp
from jax import lax
from jax.experimental import pallas as pl
from jax.experimental.pallas import tpu as pltpu
from jax.sharding import PartitionSpec as P

GROUPS = 32
EPS = 1e-06
F32 = jnp.float32
BF16 = jnp.bfloat16
VMEM = pl.BlockSpec(memory_space=pltpu.VMEM)
cat = jnp.concatenate


def iota(shape, dim):
    return lax.broadcasted_iota(jnp.int32, shape, dim)


def exact_dot(rows, zero_one):
    n = rows.shape[0]
    high = rows.astype(BF16)
    rest = rows - high.astype(F32)
    middle = rest.astype(BF16)
    low = (rest - middle.astype(F32)).astype(BF16)
    parts = cat([high.astype(F32), middle.astype(F32), low.astype(F32)], axis=0)
    spare = -parts.shape[0] % 16
    if spare:
        parts = cat([parts, jnp.zeros((spare, parts.shape[1]), F32)], axis=0)
    found = jnp.dot(parts.astype(BF16), zero_one.astype(BF16), preferred_element_type=F32)
    return found[:n] + found[n : 2 * n] + found[2 * n : 3 * n]


def group_matrix(channels):
    size = channels // GROUPS
    return (iota((channels, 128), 0) // size == iota((channels, 128), 1) % GROUPS).astype(F32)


def matrix_kernel(out_ref):
    out_ref[...] = group_matrix(out_ref.shape[0])


def pack_row(sums, gather=None):
    channels = sums[0].shape[1]
    if gather is None:
        gather = group_matrix(channels)
    grouped = exact_dot(cat(sums, axis=0), gather)
    place = iota((4, 128), 1) // GROUPS == iota((4, 128), 0)
    return jnp.sum(jnp.where(place, grouped, 0.0), axis=0, keepdims=True)


def frame_sums(lines):
    deep = 64
    channels = lines[0].shape[1]
    one, two = jnp.zeros((deep, channels), F32), jnp.zeros((deep, channels), F32)
    for v in lines:
        for a in range(0, v.shape[0], deep):
            part = v[a : a + deep]
            one, two = one + part, two + part * part
    return [jnp.sum(one, axis=0, keepdims=True), jnp.sum(two, axis=0, keepdims=True)]


def scale_and_shift(rows, info_ref, gain, offset, cells, bands):
    channels = gain.shape[1]
    size = channels // GROUPS
    frame = 2 * (iota(rows.shape, 0) // bands) + iota(rows.shape, 1) // 64
    lane, channel = iota((128, 2 * channels), 0) % 64, iota((128, 2 * channels), 1)
    spread = lane == GROUPS * (channel // channels) + channel % channels // size
    totals = []
    for n in range(2):
        begin, end = info_ref[n : n + 1, :], info_ref[4 + n : 5 + n, :]
        inside = jnp.where((frame >= begin) & (frame < end), rows, 0.0)
        totals.append(jnp.sum(inside, axis=0, keepdims=True))
    sums = exact_dot(cat(totals, axis=0), spread.astype(F32))
    found = []
    for n in range(2):
        frames = (info_ref[4 + n : 5 + n, :] - info_ref[n : n + 1, :]).astype(F32)
        per = 1.0 / (cat([frames] * (channels // 128), axis=1) * cells)
        mean = sums[n : n + 1, :channels] * per
        inv_std = lax.rsqrt(sums[n : n + 1, channels:] * per - mean * mean + EPS)
        scale = inv_std * gain
        found.append((scale, offset - mean * scale))
    return found


def sums_kernel(x_ref, gather_ref, row_ref, top_ref):
    frames, rows = x_ref.shape[:2]
    top_ref[...] = x_ref[:, 0:2]
    sums = []
    for f in range(frames):
        sums += frame_sums([x_ref[f, r].astype(F32) for r in range(rows)])
    row_ref[...] = jnp.broadcast_to(pack_row(sums, gather_ref[...])[None], row_ref.shape)


def arrange(weight_ref, weights, pairs):
    channels = weight_ref.shape[2]
    zero = jnp.zeros((channels, channels), BF16)
    for tap in range(9):
        w0, w1, w2 = (weight_ref[tap, dx] for dx in range(3))
        weights[tap, 0:channels] = cat([w1, w0], axis=1)
        weights[tap, channels : 2 * channels] = cat([w2, w1], axis=1)
    for side in range(2):
        for k in range(3):
            w0, w1, w2 = (weight_ref[k * 3 + dy, 2 * side] for dy in range(3))
            for j, blocks in enumerate(((w0, zero), (w1, w0), (w2, w1), (zero, w2))):
                at = (k * 4 + j) * channels
                pairs[side, at : at + channels] = cat(blocks, axis=1)


def clip_table(clip_ref, first):
    ids = clip_ref[...].astype(F32)
    lane = iota(ids.shape, 1)
    begins, ends = [], []
    for n in range(4):
        at = jnp.minimum(first + n, ids.shape[1] - 1)
        mine = jnp.sum(jnp.where(lane == at, ids, 0.0), axis=1, keepdims=True)
        begins.append(jnp.sum(jnp.where(ids < mine, 1.0, 0.0), axis=1, keepdims=True))
        ends.append(jnp.sum(jnp.where(ids <= mine, 1.0, 0.0), axis=1, keepdims=True))
    return cat([jnp.broadcast_to(v, (1, 128)) for v in begins + ends], axis=0).astype(jnp.int32)


def activated(value, scale, shift):
    u = value.astype(F32) * scale + shift
    return u + u * jnp.tanh(u)


def convolve(line, weight_ref, weights, pairs, sources, rows):
    wide = weights.shape[2]
    channels = wide // 2
    taps = [(k, dy) for k in range(3) for dy in (-1, 0, 1)]
    dot = functools.partial(jnp.dot, preferred_element_type=F32)

    def window(picked, lanes):
        return cat(
            [cat([line(sources[k], r, dy)[:, lanes] for r in picked], axis=0) for k, dy in taps], axis=1
        )

    total = dot(window(range(1, rows + 1), slice(0, wide)), weights[...].reshape(-1, wide))
    half = total.shape[0] // rows
    firsts, singles = range(1, rows - 2, 2), (rows - 1, rows)
    crossing = [[] for _ in range(rows)]
    for side in range(2):
        lanes = slice(channels, wide) if side == 0 else slice(0, channels)
        four = cat(
            [
                cat([line(sources[k], r + j // 3, min(j, 2) - 1)[:, lanes] for r in firsts], axis=0)
                for k in range(3)
                for j in range(4)
            ],
            axis=1,
        )
        alone = cat([weight_ref[tap, 2 * side] for tap in range(9)], axis=0)
        by_two, by_one = dot(four, pairs[side]), dot(window(singles, lanes), alone)
        shift = from_left if side == 0 else from_right
        by_two, by_one = shift(by_two, half), shift(by_one, half)
        for n in range(rows - 2):
            at = n // 2 * half
            crossing[n].append(by_two[at : at + half, n % 2 * channels : (n % 2 + 1) * channels])
        for n in range(2):
            crossing[rows - 2 + n].append(by_one[n * half : (n + 1) * half])
    return [total[n * half : (n + 1) * half] + cat(crossing[n], axis=1) for n in range(rows)]


def from_left(value, half):
    column = iota(value.shape, 0) % half
    return jnp.where(column == 0, 0.0, pltpu.roll(value, 1, 0))


def from_right(value, half):
    column = iota(value.shape, 0) % half
    return jnp.where(column == half - 1, 0.0, pltpu.roll(value, value.shape[0] - 1, 0))


def tap_weights(down_ref, k, dy):
    channels = down_ref.shape[0] // 27
    at = (k * 9 + dy * 3) * channels
    return down_ref[at : at + 2 * channels], down_ref[at + 2 * channels : at + 3 * channels]


def strided(residual_ref, frames, down_ref, k):
    rows, half, wide = residual_ref.shape[1] - 1, *residual_ref.shape[2:]
    channels = wide // 2

    def lines(picked):
        return cat([residual_ref[f, r - 1] for f in frames for r in picked], axis=0)

    zero, one = lines(range(2, rows, 2)), lines(range(1, rows, 2))
    two = lines([*range(2, rows, 2), rows + 1])
    (both_0, next_0), (both_1, next_1), (both_2, next_2) = (tap_weights(down_ref, k, dy) for dy in range(3))
    dot = functools.partial(jnp.dot, preferred_element_type=F32)
    total = dot(cat([one, two], axis=1), cat([both_1, both_2], axis=0))
    evens = cat([one[:, :channels], two[:, :channels]], axis=1)
    total = total + from_right(dot(evens, cat([next_1, next_2], axis=0)), half)
    upper = dot(zero, both_0) + from_right(dot(zero[:, :channels], next_0), half)
    total = total.reshape(len(frames), rows // 2, half, -1)
    upper = upper.reshape(len(frames), rows // 2 - 1, half, -1)
    return cat([total[:, :1], total[:, 1:] + upper], axis=1)


def hand_on(residual_ref, info_ref, first, down_ref, partial_ref):
    begins = [info_ref[2, 0], info_ref[3, 0]]
    source = (begins[0] > first).astype(jnp.int32)
    takes = [(b <= first + 1).astype(F32) for b in begins]
    older = strided(residual_ref, (source, 1), down_ref, 0)
    newer = strided(residual_ref, (1,), down_ref, 1)
    partial_ref[0] = ((older[0] + newer[0]) * takes[0]).astype(BF16)
    partial_ref[1] = (older[1] * takes[1]).astype(BF16)


def frame_sources(info_ref, first):
    return [
        [jnp.maximum(first + f - 2 + k, info_ref[f, 0]) - (first - 2) for k in range(3)] for f in range(2)
    ]


def on_core(which):
    return pl.when(lax.axis_index("tm") % 2 == which)


def second_core_kernel(bands, cells, down_ref, clip_ref, *refs):
    ins, (residual_ref, edge_ref, partial_ref, info_ref), scratch = refs[:9], refs[9:13], refs[13:]
    first = lax.axis_index("tm") * 2
    info_ref[...] = clip_table(clip_ref, first)

    @on_core(1)
    def _():
        convolve_frames(bands, cells, info_ref, *ins, residual_ref, edge_ref, *scratch)
        hand_on(residual_ref, info_ref, first, down_ref, partial_ref)


def first_core_kernel(bands, cells, other_edge_ref, info_ref, *refs):
    ins, (residual_ref, edge_ref), scratch = refs[:9], refs[9:11], refs[11:]

    @on_core(0)
    def _():
        convolve_frames(bands, cells, info_ref, *ins, residual_ref, edge_ref, *scratch)

    @on_core(1)
    def _():
        edge_ref[...] = other_edge_ref[...]


def convolve_frames(
    bands, cells, info_ref, rows_ref, bias_ref, gain_ref, offset_ref, weight_ref,
    x_ref, before_ref, below_ref, below_before_ref,
    residual_ref, edge_ref, hidden, own, weights, pairs, slots,
):
    rows, cols, channels = x_ref.shape[1:]
    first = lax.axis_index("tm") * 2
    keep = (lax.axis_index("band") < bands - 1).astype(F32)
    arrange(weight_ref, weights, pairs)
    bias = bias_ref[...]
    stats = scale_and_shift(rows_ref[...], info_ref, gain_ref[...], offset_ref[...], cells, bands)
    stats = [0.5 * v for pair in stats for v in pair]
    for frame in range(4):
        scale, shift = stats[2:] if frame == 3 else stats[:2]
        body, below = (before_ref, below_before_ref) if frame < 2 else (x_ref, below_ref)
        f = frame % 2
        lines = [body.at[f, r] for r in range(rows)] + [below.at[f, r] for r in range(2)]
        for n, line in enumerate(lines):
            slot = slots.at[n]
            slot[...] = line[...].astype(F32)
            for side in range(2):
                lanes = pl.ds(side * channels, channels)
                value = slot[pl.ds(side, cols // 2, 2), :]
                if frame >= 2 and 1 <= n <= rows:
                    own[f, n - 1, :, lanes] = value.astype(BF16)
                value = activated(value, scale, shift)
                hidden[frame, n, :, lanes] = value.astype(BF16)
                if n in (rows - 1, rows):
                    hidden[frame, n + 3, :, lanes] = (value * keep).astype(BF16)

    def line(source, r, dy):
        across = (r, dy) in ((rows - 1, 1), (rows, -1))
        return hidden[source, r + dy + (3 if across else 0)]

    sources = frame_sources(info_ref, first)
    bias = cat([bias, bias], axis=1)
    for f in range(2):
        found = convolve(line, weight_ref, weights, pairs, sources[f], rows)
        for n, total in enumerate(found):
            value = total + own[f, n].astype(F32) + bias
            residual_ref[f, n] = value.astype(BF16)
            if n == rows - 1:
                residual_ref[f, rows] = (value * keep).astype(BF16)
                edge_ref[f] = value.astype(BF16)


def hand_on_kernel(info_ref, residual_ref, down_ref, partial_ref):
    @on_core(0)
    def _():
        hand_on(residual_ref, info_ref, lax.axis_index("tm") * 2, down_ref, partial_ref)


def local_kernel(info_ref, first_core_ref, second_core_ref, down_ref, out_ref):
    for which, residual_ref in enumerate((first_core_ref, second_core_ref)):

        @on_core(which)
        def _(residual_ref=residual_ref):
            local_part(info_ref, residual_ref, down_ref, out_ref)


def local_part(info_ref, residual_ref, down_ref, out_ref):
    first = lax.axis_index("tm") * 2
    begins = [info_ref[0, 0], info_ref[1, 0]]
    base = strided(residual_ref, (0, 1), down_ref, 2)
    out_ref[0] = base[0]
    out_ref[1] = base[1] + strided(residual_ref, ((begins[1] > first).astype(jnp.int32),), down_ref, 1)[0]

    @pl.when(begins[0] == first)
    def _():
        out_ref[0] += strided(residual_ref, (0,), down_ref, 0)[0] + strided(residual_ref, (0,), down_ref, 1)[0]

    @pl.when(begins[1] >= first)
    def _():
        out_ref[1] += strided(residual_ref, (begins[1] - first,), down_ref, 0)[0]


def row_zero_kernel(info_ref, edge_before_ref, edge_ref, down_ref, out_ref, four):
    half, wide = edge_ref.shape[1:]
    four[0:2] = edge_before_ref[...]
    four[2:4] = edge_ref[...]
    sources = frame_sources(info_ref, lax.axis_index("tm") * 2)
    weights = [tap_weights(down_ref, k, 0) for k in range(3)]
    lines = cat([cat([four[s] for s in sources[f]], axis=1) for f in range(2)], axis=0)
    evens = cat([lines[:, k * wide : k * wide + wide // 2] for k in range(3)], axis=1)
    total = jnp.dot(lines, cat([w[0] for w in weights], axis=0), preferred_element_type=F32)
    shifted = jnp.dot(evens, cat([w[1] for w in weights], axis=0), preferred_element_type=F32)
    out_ref[...] = (total + from_right(shifted, half)).reshape(out_ref.shape)


def first_line_kernel(upper_ref, local_ref, between_ref, out_ref):
    out_ref[...] = upper_ref[...] + local_ref[:, 0] + between_ref[:, 0].astype(F32)


def join_kernel(first_line_ref, local_ref, between_ref, within_ref, reduced_ref, row_ref):
    frames, lines = local_ref.shape[:2]
    sums = []
    for f in range(frames):
        values = []
        for i in range(lines):
            v = first_line_ref[f] if i == 0 else local_ref[f, i] + between_ref[f, i].astype(F32)
            v = (v + within_ref[f, i].astype(F32)).astype(BF16)
            reduced_ref[f, i] = v
            values.append(v.astype(F32))
        sums += frame_sums(values)
    row_ref[...] = jnp.broadcast_to(pack_row(sums)[None], row_ref.shape)


def out_kernel(bands, cells, rows_ref, info_ref, gain_ref, offset_ref, reduced_ref, out_ref):
    frames, lines = reduced_ref.shape[:2]
    stats = scale_and_shift(rows_ref[...], info_ref, gain_ref[...], offset_ref[...], cells, bands)
    for f in range(frames):
        scale, shift = stats[f]
        for i in range(lines):
            out_ref[f, i] = (reduced_ref[f, i].astype(F32) * scale + shift).astype(BF16)


def call(kernel, out_shape, in_specs, scratch=(), megabytes=4, flops=0, moved=0):
    return pl.pallas_call(
        kernel,
        out_shape=out_shape,
        in_specs=in_specs,
        out_specs=jax.tree.map(lambda _: VMEM, out_shape),
        scratch_shapes=list(scratch),
        compiler_params=pltpu.CompilerParams(vmem_limit_bytes=megabytes << 20),
        cost_estimate=pl.CostEstimate(flops=flops, bytes_accessed=moved, transcendentals=0),
    )


def passed_on(array, tm_by, band_by):
    tms, bands = lax.axis_size("tm"), lax.axis_size("band")
    pairs = [
        (i * bands + b, (i + tm_by) % tms * bands + (b + band_by) % bands)
        for i in range(tms)
        for b in range(bands)
    ]
    return lax.ppermute(array, ("tm", "band"), pairs)


def between_chips(array):
    return lax.ppermute(array, "tm", [(i, i + 1) for i in range(1, lax.axis_size("tm") - 1, 2)])


def within_chips(array):
    return lax.ppermute(array, "tm", [(i, i + 1) for i in range(0, lax.axis_size("tm"), 2)])


def on_device(
    frames_in, clip_id, conv_weight, conv_bias, norm_gain, norm_shift, down_weight, out_gain, out_shift
):
    frames, rows, cols, channels = frames_in.shape
    wide = down_weight.shape[-1]
    bands = lax.axis_size("band")
    devices, half, lines = lax.axis_size("tm") * bands, cols // 2, rows // 2
    shape = jax.ShapeDtypeStruct
    everyone = shape((devices, 1, 128), F32)

    def exchange(row):
        return lax.all_to_all(row, ("tm", "band"), 0, 0, tiled=True).reshape(devices, 128)

    before = passed_on(frames_in, 1, 0)
    gather = call(matrix_kernel, shape((channels, 128), F32), [], flops=1 << 29)()
    row, top = call(
        sums_kernel,
        (everyone, shape((frames, 2, cols, channels), BF16)),
        [VMEM] * 2,
        flops=1 << 33,
        moved=1 << 20,
    )(frames_in, gather)
    below_before, below = passed_on(top, 1, -1), passed_on(top, 0, -1)
    sums = exchange(row)
    down = down_weight.reshape(-1, wide)
    pair = (half, 2 * channels)
    def conv(kernel, given, ranges, *made):
        cells = float(bands * rows * cols * (channels // GROUPS))
        return call(
            functools.partial(kernel, bands, cells),
            (shape((frames, rows + 1, *pair), BF16), shape((frames, *pair), BF16), *made),
            [VMEM] * 11,
            scratch=[
                pltpu.VMEM((4, rows + 4, *pair), BF16),
                pltpu.VMEM((frames, rows, *pair), BF16),
                pltpu.VMEM((9, 2 * channels, 2 * channels), BF16),
                pltpu.VMEM((2, 12 * channels, 2 * channels), BF16),
                pltpu.VMEM((rows + 2, cols, channels), F32),
            ],
            megabytes=24,
            flops=5 << 30,
            moved=1 << 23,
        )(
            given, ranges, sums, conv_bias.reshape(1, -1), norm_gain.reshape(1, -1), norm_shift.reshape(1, -1),
            conv_weight.reshape(9, 3, channels, channels), frames_in, before, below, below_before,
        )

    sent = shape((frames, lines, half, wide), BF16)
    second_core, edge, partial, info = conv(
        second_core_kernel, down, clip_id.reshape(1, -1), sent, shape((8, 128), jnp.int32)
    )
    between = between_chips(partial)
    first_core, edge = conv(first_core_kernel, edge, info)
    edge, edge_before = passed_on(edge, 0, 1), passed_on(edge, 1, 1)
    partial = call(hand_on_kernel, sent, [VMEM] * 3, megabytes=12, flops=1 << 30, moved=1 << 22)(
        info, first_core, down
    )
    within = within_chips(partial)
    local = call(
        local_kernel,
        shape((frames, lines, half, wide), F32),
        [VMEM] * 4,
        megabytes=12,
        flops=1 << 31,
        moved=1 << 22,
    )(info, first_core, second_core, down)
    line = shape((frames, half, wide), F32)
    upper = call(
        row_zero_kernel, line, [VMEM] * 4, scratch=[pltpu.VMEM((4, *pair), BF16)], megabytes=6
    )(info, edge_before, edge, down)
    first_line = call(first_line_kernel, line, [VMEM] * 3, flops=1 << 32)(upper, local, between)
    reduced, row = call(
        join_kernel,
        (shape((frames, lines, half, wide), BF16), everyone),
        [VMEM] * 4,
        megabytes=8,
        moved=1 << 21,
    )(first_line, local, between, within)
    return call(
        functools.partial(out_kernel, bands, float(bands * lines * half * (wide // GROUPS))),
        shape((frames, lines, half, wide), BF16),
        [VMEM] * 5,
        megabytes=8,
        moved=1 << 20,
    )(exchange(row), info, out_gain.reshape(1, -1), out_shift.reshape(1, -1), reduced)


def solution(mesh):
    return jax.shard_map(
        on_device,
        mesh=mesh,
        in_specs=(P("tm", "band", None, None), P(), P(), P(), P(), P(), P(), P(), P()),
        out_specs=P("tm", "band", None, None),
        check_vma=False,
    )
```

```python
import functools
import jax
import jax.numpy as jnp
from jax import lax
from jax.experimental import pallas as pl
from jax.experimental.pallas import tpu as pltpu
from jax.sharding import PartitionSpec as P

GROUPS = 32
EPS = 1e-06
F32 = jnp.float32
BF16 = jnp.bfloat16
VMEM = pl.BlockSpec(memory_space=pltpu.VMEM)
cat = jnp.concatenate


def iota(shape, dim):
    return lax.broadcasted_iota(jnp.int32, shape, dim)


def exact_dot(rows, zero_one):
    n = rows.shape[0]
    high = rows.astype(BF16)
    rest = rows - high.astype(F32)
    middle = rest.astype(BF16)
    low = (rest - middle.astype(F32)).astype(BF16)
    parts = cat([high.astype(F32), middle.astype(F32), low.astype(F32)], axis=0)
    spare = -parts.shape[0] % 16
    if spare:
        parts = cat([parts, jnp.zeros((spare, parts.shape[1]), F32)], axis=0)
    found = jnp.dot(parts.astype(BF16), zero_one.astype(BF16), preferred_element_type=F32)
    return found[:n] + found[n : 2 * n] + found[2 * n : 3 * n]


def group_matrix(channels):
    size = channels // GROUPS
    return (iota((channels, 128), 0) // size == iota((channels, 128), 1) % GROUPS).astype(F32)


def matrix_kernel(out_ref):
    out_ref[...] = group_matrix(out_ref.shape[0])


def pack_row(sums, gather=None):
    channels = sums[0].shape[1]
    if gather is None:
        gather = group_matrix(channels)
    grouped = exact_dot(cat(sums, axis=0), gather)
    place = iota((4, 128), 1) // GROUPS == iota((4, 128), 0)
    return jnp.sum(jnp.where(place, grouped, 0.0), axis=0, keepdims=True)


def frame_sums(lines):
    deep = 64
    channels = lines[0].shape[1]
    one, two = jnp.zeros((deep, channels), F32), jnp.zeros((deep, channels), F32)
    for v in lines:
        for a in range(0, v.shape[0], deep):
            part = v[a : a + deep]
            one, two = one + part, two + part * part
    return [jnp.sum(one, axis=0, keepdims=True), jnp.sum(two, axis=0, keepdims=True)]


def scale_and_shift(rows, info_ref, gain, offset, cells, bands):
    channels = gain.shape[1]
    size = channels // GROUPS
    frame = 2 * (iota(rows.shape, 0) // bands) + iota(rows.shape, 1) // 64
    lane, channel = iota((128, 2 * channels), 0) % 64, iota((128, 2 * channels), 1)
    spread = lane == GROUPS * (channel // channels) + channel % channels // size
    totals = []
    for n in range(2):
        begin, end = info_ref[n : n + 1, :], info_ref[4 + n : 5 + n, :]
        inside = jnp.where((frame >= begin) & (frame < end), rows, 0.0)
        totals.append(jnp.sum(inside, axis=0, keepdims=True))
    sums = exact_dot(cat(totals, axis=0), spread.astype(F32))
    found = []
    for n in range(2):
        frames = (info_ref[4 + n : 5 + n, :] - info_ref[n : n + 1, :]).astype(F32)
        per = 1.0 / (cat([frames] * (channels // 128), axis=1) * cells)
        mean = sums[n : n + 1, :channels] * per
        inv_std = lax.rsqrt(sums[n : n + 1, channels:] * per - mean * mean + EPS)
        scale = inv_std * gain
        found.append((scale, offset - mean * scale))
    return found


def sums_kernel(x_ref, gather_ref, row_ref, top_ref):
    frames, rows = x_ref.shape[:2]
    top_ref[...] = x_ref[:, 0:2]
    sums = []
    for f in range(frames):
        sums += frame_sums([x_ref[f, r].astype(F32) for r in range(rows)])
    row_ref[...] = jnp.broadcast_to(pack_row(sums, gather_ref[...])[None], row_ref.shape)


def arrange(weight_ref, weights, pairs):
    channels = weight_ref.shape[2]
    zero = jnp.zeros((channels, channels), BF16)
    for tap in range(9):
        w0, w1, w2 = (weight_ref[tap, dx] for dx in range(3))
        weights[tap, 0:channels] = cat([w1, w0], axis=1)
        weights[tap, channels : 2 * channels] = cat([w2, w1], axis=1)
    for side in range(2):
        for k in range(3):
            w0, w1, w2 = (weight_ref[k * 3 + dy, 2 * side] for dy in range(3))
            for j, blocks in enumerate(((w0, zero), (w1, w0), (w2, w1), (zero, w2))):
                at = (k * 4 + j) * channels
                pairs[side, at : at + channels] = cat(blocks, axis=1)


def clip_table(clip_ref, first):
    ids = clip_ref[...].astype(F32)
    lane = iota(ids.shape, 1)
    begins, ends = [], []
    for n in range(4):
        at = jnp.minimum(first + n, ids.shape[1] - 1)
        mine = jnp.sum(jnp.where(lane == at, ids, 0.0), axis=1, keepdims=True)
        begins.append(jnp.sum(jnp.where(ids < mine, 1.0, 0.0), axis=1, keepdims=True))
        ends.append(jnp.sum(jnp.where(ids <= mine, 1.0, 0.0), axis=1, keepdims=True))
    return cat([jnp.broadcast_to(v, (1, 128)) for v in begins + ends], axis=0).astype(jnp.int32)


def activated(value, scale, shift):
    u = value.astype(F32) * scale + shift
    return u + u * jnp.tanh(u)


def convolve(line, weight_ref, weights, pairs, sources, rows):
    wide = weights.shape[2]
    channels = wide // 2
    taps = [(k, dy) for k in range(3) for dy in (-1, 0, 1)]
    dot = functools.partial(jnp.dot, preferred_element_type=F32)

    def window(picked, lanes):
        return cat(
            [cat([line(sources[k], r, dy)[:, lanes] for r in picked], axis=0) for k, dy in taps], axis=1
        )

    total = dot(window(range(1, rows + 1), slice(0, wide)), weights[...].reshape(-1, wide))
    half = total.shape[0] // rows
    firsts, singles = range(1, rows - 2, 2), (rows - 1, rows)
    crossing = [[] for _ in range(rows)]
    for side in range(2):
        lanes = slice(channels, wide) if side == 0 else slice(0, channels)
        four = cat(
            [
                cat([line(sources[k], r + j // 3, min(j, 2) - 1)[:, lanes] for r in firsts], axis=0)
                for k in range(3)
                for j in range(4)
            ],
            axis=1,
        )
        alone = cat([weight_ref[tap, 2 * side] for tap in range(9)], axis=0)
        by_two, by_one = dot(four, pairs[side]), dot(window(singles, lanes), alone)
        shift = from_left if side == 0 else from_right
        by_two, by_one = shift(by_two, half), shift(by_one, half)
        for n in range(rows - 2):
            at = n // 2 * half
            crossing[n].append(by_two[at : at + half, n % 2 * channels : (n % 2 + 1) * channels])
        for n in range(2):
            crossing[rows - 2 + n].append(by_one[n * half : (n + 1) * half])
    return [total[n * half : (n + 1) * half] + cat(crossing[n], axis=1) for n in range(rows)]


def from_left(value, half):
    column = iota(value.shape, 0) % half
    return jnp.where(column == 0, 0.0, pltpu.roll(value, 1, 0))


def from_right(value, half):
    column = iota(value.shape, 0) % half
    return jnp.where(column == half - 1, 0.0, pltpu.roll(value, value.shape[0] - 1, 0))


def tap_weights(down_ref, k, dy):
    channels = down_ref.shape[0] // 27
    at = (k * 9 + dy * 3) * channels
    return down_ref[at : at + 2 * channels], down_ref[at + 2 * channels : at + 3 * channels]


def strided(residual_ref, frames, down_ref, k):
    rows, half, wide = residual_ref.shape[1] - 1, *residual_ref.shape[2:]
    channels = wide // 2

    def lines(picked):
        return cat([residual_ref[f, r - 1] for f in frames for r in picked], axis=0)

    zero, one = lines(range(2, rows, 2)), lines(range(1, rows, 2))
    two = lines([*range(2, rows, 2), rows + 1])
    (both_0, next_0), (both_1, next_1), (both_2, next_2) = (tap_weights(down_ref, k, dy) for dy in range(3))
    dot = functools.partial(jnp.dot, preferred_element_type=F32)
    total = dot(cat([one, two], axis=1), cat([both_1, both_2], axis=0))
    evens = cat([one[:, :channels], two[:, :channels]], axis=1)
    total = total + from_right(dot(evens, cat([next_1, next_2], axis=0)), half)
    upper = dot(zero, both_0) + from_right(dot(zero[:, :channels], next_0), half)
    total = total.reshape(len(frames), rows // 2, half, -1)
    upper = upper.reshape(len(frames), rows // 2 - 1, half, -1)
    return cat([total[:, :1], total[:, 1:] + upper], axis=1)


def hand_on(residual_ref, info_ref, first, down_ref, partial_ref):
    begins = [info_ref[2, 0], info_ref[3, 0]]
    source = (begins[0] > first).astype(jnp.int32)
    takes = [(b <= first + 1).astype(F32) for b in begins]
    older = strided(residual_ref, (source, 1), down_ref, 0)
    newer = strided(residual_ref, (1,), down_ref, 1)
    partial_ref[0] = ((older[0] + newer[0]) * takes[0]).astype(BF16)
    partial_ref[1] = (older[1] * takes[1]).astype(BF16)


def frame_sources(info_ref, first):
    return [
        [jnp.maximum(first + f - 2 + k, info_ref[f, 0]) - (first - 2) for k in range(3)] for f in range(2)
    ]


def on_core(which):
    return pl.when(lax.axis_index("tm") % 2 == which)


def second_core_kernel(bands, cells, down_ref, clip_ref, *refs):
    ins, (residual_ref, edge_ref, partial_ref, info_ref), scratch = refs[:9], refs[9:13], refs[13:]
    first = lax.axis_index("tm") * 2
    info_ref[...] = clip_table(clip_ref, first)

    @on_core(1)
    def _():
        convolve_frames(bands, cells, info_ref, *ins, residual_ref, edge_ref, *scratch)
        hand_on(residual_ref, info_ref, first, down_ref, partial_ref)


def first_core_kernel(bands, cells, other_edge_ref, info_ref, *refs):
    ins, (residual_ref, edge_ref), scratch = refs[:9], refs[9:11], refs[11:]

    @on_core(0)
    def _():
        convolve_frames(bands, cells, info_ref, *ins, residual_ref, edge_ref, *scratch)

    @on_core(1)
    def _():
        edge_ref[...] = other_edge_ref[...]


def convolve_frames(
    bands, cells, info_ref, rows_ref, bias_ref, gain_ref, offset_ref, weight_ref,
    x_ref, before_ref, below_ref, below_before_ref,
    residual_ref, edge_ref, hidden, own, weights, pairs, slots,
):
    rows, cols, channels = x_ref.shape[1:]
    first = lax.axis_index("tm") * 2
    keep = (lax.axis_index("band") < bands - 1).astype(F32)
    arrange(weight_ref, weights, pairs)
    bias = bias_ref[...]
    stats = scale_and_shift(rows_ref[...], info_ref, gain_ref[...], offset_ref[...], cells, bands)
    stats = [0.5 * v for pair in stats for v in pair]
    for frame in range(4):
        scale, shift = stats[2:] if frame == 3 else stats[:2]
        body, below = (before_ref, below_before_ref) if frame < 2 else (x_ref, below_ref)
        f = frame % 2
        lines = [body.at[f, r] for r in range(rows)] + [below.at[f, r] for r in range(2)]
        for n, line in enumerate(lines):
            slot = slots.at[n]
            slot[...] = line[...].astype(F32)
            for side in range(2):
                lanes = pl.ds(side * channels, channels)
                value = slot[pl.ds(side, cols // 2, 2), :]
                if frame >= 2 and 1 <= n <= rows:
                    own[f, n - 1, :, lanes] = value.astype(BF16)
                value = activated(value, scale, shift)
                hidden[frame, n, :, lanes] = value.astype(BF16)
                if n in (rows - 1, rows):
                    hidden[frame, n + 3, :, lanes] = (value * keep).astype(BF16)

    def line(source, r, dy):
        across = (r, dy) in ((rows - 1, 1), (rows, -1))
        return hidden[source, r + dy + (3 if across else 0)]

    sources = frame_sources(info_ref, first)
    bias = cat([bias, bias], axis=1)
    for f in range(2):
        found = convolve(line, weight_ref, weights, pairs, sources[f], rows)
        for n, total in enumerate(found):
            value = total + own[f, n].astype(F32) + bias
            residual_ref[f, n] = value.astype(BF16)
            if n == rows - 1:
                residual_ref[f, rows] = (value * keep).astype(BF16)
                edge_ref[f] = value.astype(BF16)


def hand_on_kernel(info_ref, residual_ref, down_ref, partial_ref):
    @on_core(0)
    def _():
        hand_on(residual_ref, info_ref, lax.axis_index("tm") * 2, down_ref, partial_ref)


def local_kernel(info_ref, first_core_ref, second_core_ref, down_ref, out_ref):
    for which, residual_ref in enumerate((first_core_ref, second_core_ref)):

        @on_core(which)
        def _(residual_ref=residual_ref):
            local_part(info_ref, residual_ref, down_ref, out_ref)


def local_part(info_ref, residual_ref, down_ref, out_ref):
    first = lax.axis_index("tm") * 2
    begins = [info_ref[0, 0], info_ref[1, 0]]
    base = strided(residual_ref, (0, 1), down_ref, 2)
    out_ref[0] = base[0]
    out_ref[1] = base[1] + strided(residual_ref, ((begins[1] > first).astype(jnp.int32),), down_ref, 1)[0]

    @pl.when(begins[0] == first)
    def _():
        out_ref[0] += strided(residual_ref, (0,), down_ref, 0)[0] + strided(residual_ref, (0,), down_ref, 1)[0]

    @pl.when(begins[1] >= first)
    def _():
        out_ref[1] += strided(residual_ref, (begins[1] - first,), down_ref, 0)[0]


def row_zero_kernel(info_ref, edge_ref, edge_before_ref, down_ref, out_ref, four):
    half, wide = edge_ref.shape[1:]
    four[0:2] = edge_before_ref[...]
    four[2:4] = edge_ref[...]
    sources = frame_sources(info_ref, lax.axis_index("tm") * 2)
    weights = [tap_weights(down_ref, k, 0) for k in range(3)]
    lines = cat([cat([four[s] for s in sources[f]], axis=1) for f in range(2)], axis=0)
    evens = cat([lines[:, k * wide : k * wide + wide // 2] for k in range(3)], axis=1)
    total = jnp.dot(lines, cat([w[0] for w in weights], axis=0), preferred_element_type=F32)
    shifted = jnp.dot(evens, cat([w[1] for w in weights], axis=0), preferred_element_type=F32)
    out_ref[...] = (total + from_right(shifted, half)).reshape(out_ref.shape)


def first_line_kernel(upper_ref, local_ref, between_ref, out_ref):
    out_ref[...] = upper_ref[...] + local_ref[:, 0] + between_ref[:, 0].astype(F32)


def join_kernel(first_line_ref, local_ref, between_ref, within_ref, reduced_ref, row_ref):
    frames, lines = local_ref.shape[:2]
    sums = []
    for f in range(frames):
        values = []
        for i in range(lines):
            v = first_line_ref[f] if i == 0 else local_ref[f, i] + between_ref[f, i].astype(F32)
            v = (v + within_ref[f, i].astype(F32)).astype(BF16)
            reduced_ref[f, i] = v
            values.append(v.astype(F32))
        sums += frame_sums(values)
    row_ref[...] = jnp.broadcast_to(pack_row(sums)[None], row_ref.shape)


def out_kernel(bands, cells, rows_ref, info_ref, gain_ref, offset_ref, reduced_ref, out_ref):
    frames, lines = reduced_ref.shape[:2]
    stats = scale_and_shift(rows_ref[...], info_ref, gain_ref[...], offset_ref[...], cells, bands)
    for f in range(frames):
        scale, shift = stats[f]
        for i in range(lines):
            out_ref[f, i] = (reduced_ref[f, i].astype(F32) * scale + shift).astype(BF16)


def call(kernel, out_shape, in_specs, scratch=(), megabytes=4, flops=0, moved=0):
    return pl.pallas_call(
        kernel,
        out_shape=out_shape,
        in_specs=in_specs,
        out_specs=jax.tree.map(lambda _: VMEM, out_shape),
        scratch_shapes=list(scratch),
        compiler_params=pltpu.CompilerParams(vmem_limit_bytes=megabytes << 20),
        cost_estimate=pl.CostEstimate(flops=flops, bytes_accessed=moved, transcendentals=0),
    )


def passed_on(array, tm_by, band_by):
    tms, bands = lax.axis_size("tm"), lax.axis_size("band")
    pairs = [
        (i * bands + b, (i + tm_by) % tms * bands + (b + band_by) % bands)
        for i in range(tms)
        for b in range(bands)
    ]
    return lax.ppermute(array, ("tm", "band"), pairs)


def between_chips(array):
    return lax.ppermute(array, "tm", [(i, i + 1) for i in range(1, lax.axis_size("tm") - 1, 2)])


def within_chips(array):
    return lax.ppermute(array, "tm", [(i, i + 1) for i in range(0, lax.axis_size("tm"), 2)])


def on_device(
    frames_in, clip_id, conv_weight, conv_bias, norm_gain, norm_shift, down_weight, out_gain, out_shift
):
    frames, rows, cols, channels = frames_in.shape
    wide = down_weight.shape[-1]
    bands = lax.axis_size("band")
    devices, half, lines = lax.axis_size("tm") * bands, cols // 2, rows // 2
    shape = jax.ShapeDtypeStruct
    everyone = shape((devices, 1, 128), F32)

    def exchange(row):
        return lax.all_to_all(row, ("tm", "band"), 0, 0, tiled=True).reshape(devices, 128)

    before = passed_on(frames_in, 1, 0)
    gather = call(matrix_kernel, shape((channels, 128), F32), [], flops=1 << 29)()
    row, top = call(
        sums_kernel,
        (everyone, shape((frames, 2, cols, channels), BF16)),
        [VMEM] * 2,
        flops=1 << 33,
        moved=1 << 20,
    )(frames_in, gather)
    below_before, below = passed_on(top, 1, -1), passed_on(top, 0, -1)
    sums = exchange(row)
    down = down_weight.reshape(-1, wide)
    pair = (half, 2 * channels)
    def conv(kernel, given, ranges, *made):
        cells = float(bands * rows * cols * (channels // GROUPS))
        return call(
            functools.partial(kernel, bands, cells),
            (shape((frames, rows + 1, *pair), BF16), shape((frames, *pair), BF16), *made),
            [VMEM] * 11,
            scratch=[
                pltpu.VMEM((4, rows + 4, *pair), BF16),
                pltpu.VMEM((frames, rows, *pair), BF16),
                pltpu.VMEM((9, 2 * channels, 2 * channels), BF16),
                pltpu.VMEM((2, 12 * channels, 2 * channels), BF16),
                pltpu.VMEM((rows + 2, cols, channels), F32),
            ],
            megabytes=24,
            flops=5 << 30,
            moved=1 << 23,
        )(
            given, ranges, sums, conv_bias.reshape(1, -1), norm_gain.reshape(1, -1), norm_shift.reshape(1, -1),
            conv_weight.reshape(9, 3, channels, channels), frames_in, before, below, below_before,
        )

    sent = shape((frames, lines, half, wide), BF16)
    second_core, edge, partial, info = conv(
        second_core_kernel, down, clip_id.reshape(1, -1), sent, shape((8, 128), jnp.int32)
    )
    between = between_chips(partial)
    first_core, edge = conv(first_core_kernel, edge, info)
    edge, edge_before = passed_on(edge, 0, 1), passed_on(edge, 1, 1)
    partial = call(hand_on_kernel, sent, [VMEM] * 3, megabytes=12, flops=1 << 30, moved=1 << 22)(
        info, first_core, down
    )
    within = within_chips(partial)
    local = call(
        local_kernel,
        shape((frames, lines, half, wide), F32),
        [VMEM] * 4,
        megabytes=12,
        flops=1 << 31,
        moved=1 << 22,
    )(info, first_core, second_core, down)
    line = shape((frames, half, wide), F32)
    upper = call(
        row_zero_kernel, line, [VMEM] * 4, scratch=[pltpu.VMEM((4, *pair), BF16)], megabytes=6
    )(info, edge, edge_before, down)
    first_line = call(first_line_kernel, line, [VMEM] * 3, flops=1 << 32)(upper, local, between)
    reduced, row = call(
        join_kernel,
        (shape((frames, lines, half, wide), BF16), everyone),
        [VMEM] * 4,
        megabytes=8,
        moved=1 << 21,
    )(first_line, local, between, within)
    return call(
        functools.partial(out_kernel, bands, float(bands * lines * half * (wide // GROUPS))),
        shape((frames, lines, half, wide), BF16),
        [VMEM] * 5,
        megabytes=8,
        moved=1 << 20,
    )(exchange(row), info, out_gain.reshape(1, -1), out_shift.reshape(1, -1), reduced)


def solution(mesh):
    return jax.shard_map(
        on_device,
        mesh=mesh,
        in_specs=(P("tm", "band", None, None), P(), P(), P(), P(), P(), P(), P(), P()),
        out_specs=P("tm", "band", None, None),
        check_vma=False,
    )
```
